32 devices in a mesh: ctx: 4 (over y, x), head: 4 (over z), dp: 2 (over core).
Axes of the slice: x: 2, y: 2, z: 4, core: 2. Of those that a mesh axis runs over, the one named last changes fastest.
Arguments:
- queries: bfloat16 [2, 1024, 4096], P('dp', 'ctx', 'head'), may hold values from -6 to 6
- keys: bfloat16 [2, 1024, 4096], P('dp', 'ctx', 'head'), may hold values from -6 to 6
- values: bfloat16 [2, 1024, 4096], P('dp', 'ctx', 'head'), may hold values from -6 to 6
- log_decay: float32 [2, 32, 1024], P('dp', 'head', 'ctx'), may hold values from -1.5 to 0
- w_out: bfloat16 [128, 32, 3072], P(('ctx', 'dp'), 'head'), may hold values from -0.09375 to 0.09375
- grad_out: bfloat16 [2, 1024, 3072], P('dp', 'ctx'), may hold values from -6 to 6
Outputs:
- mixed: bfloat16 [2, 1024, 3072], P('dp', 'ctx', 'head')
- query_grad: bfloat16 [2, 1024, 4096], P('dp', 'ctx', 'head')
- key_grad: bfloat16 [2, 1024, 4096], P('dp', 'ctx', 'head')
- value_grad: bfloat16 [2, 1024, 4096], P('dp', 'ctx', 'head')
- w_grad: float32 [128, 32, 3072], P(('ctx', 'dp'), 'head')
The draws below stay inside these ranges and needn't reach their ends.
All inputs are finite; a program needn't handle non-finite values.
Results may differ from the reference program's by a relative error of at most 0.015.
Values may be sent and summed in bfloat16 or wider, within the bound.
No kernel may reach another device: no remote copies, remote signals or barrier semaphores. Data moves between devices by JAX's collectives and lax.ppermute only.
A program may use at most 128 MiB of HBM per device.

```python
import jax
import jax.numpy as jnp
from jax import lax

H = 32
DH = 128
DOUT = 3072
BLOCK = 256
LENGTH = 1024
SEQS = 2


def draw_log_decay(key, part):
    streams = jax.random.split(key, 7)
    slow_count = 4
    slow = jax.random.randint(streams[0], (SEQS, H, 1, 1), 0, 8) < slow_count
    quick_decay_rate = jnp.exp(jax.random.uniform(streams[1], (SEQS, H, 1, 1), jnp.float32, jnp.log(1.0 / 50.0), jnp.log(1.0 / 30.0)))
    slow_rate = jnp.exp(jax.random.uniform(streams[2], (SEQS, H, 1, 1), jnp.float32, jnp.log(0.05 / LENGTH), jnp.log(0.5 / LENGTH)))
    base = jnp.where(slow, slow_rate, quick_decay_rate)
    block_total = LENGTH // BLOCK
    tile_shrinkage = jnp.exp(jax.random.uniform(streams[3], (SEQS, H, block_total, 1), jnp.float32, jnp.log(0.5), jnp.log(2.0)))
    place_factor = jnp.exp(jax.random.uniform(streams[4], (SEQS, H, block_total, BLOCK), jnp.float32, jnp.log(0.5), jnp.log(2.0)))
    fading_speed = (base * tile_shrinkage * place_factor).reshape(SEQS, H, LENGTH)
    spots = jax.random.randint(streams[5], (SEQS, H, 3, 1), 0, LENGTH)
    learning_loss = jax.random.uniform(streams[6], (SEQS, H, 3, 1), jnp.float32, 0.2, 0.35)
    agreeing_tally = spots == jnp.arange(LENGTH)[None, None, None, :]
    packet_batches = jnp.sum(jnp.where(agreeing_tally, jnp.log(1.0 - learning_loss), 0.0), axis=2)
    return (packet_batches - fading_speed).astype(jnp.float32)


def levels(rng, extent, cuts, smallest, largest):
    def one(dim, parts):
        steps = jax.random.uniform(jax.random.fold_in(jax.random.fold_in(rng, 6), dim), (parts,), jnp.float32, smallest / len(cuts), largest / len(cuts))
        return jnp.repeat(jnp.exp(steps), extent[dim] // parts).reshape((-1,) + (1,) * (len(extent) - dim - 1))

    gain = one(*cuts[0])
    for cut in cuts[1:]:
        gain = gain * one(*cut)
    return gain


def noise(key, shape, deviation, reach, pieces=(), held_as=jnp.bfloat16):
    values = deviation * jax.random.normal(key, shape, jnp.float32)
    if pieces:
        values = values * levels(key, shape, pieces, -0.22, 0.18)
    return jnp.clip(values, -reach, reach).astype(held_as)


def setup_inputs(seed: int = 0) -> dict:
    seeds = jax.random.split(jax.random.key(seed), 7)
    queries = noise(seeds[0], (SEQS, LENGTH, H * DH), 1.0, 6.0, ((0, 2), (1, 4), (2, 4)))
    keys = noise(seeds[1], (SEQS, LENGTH, H * DH), 1.0, 6.0, ((0, 2), (1, 4), (2, 4)))
    values = noise(seeds[2], (SEQS, LENGTH, H * DH), 1.0, 6.0, ((0, 2), (1, 4), (2, 4)))
    log_decay = draw_log_decay(jax.random.fold_in(seeds[6], 71), 0)
    w_out = noise(seeds[4], (DH, H, DOUT), (H * DH) ** -0.5, 0.09375, ((0, 8), (1, 4)))
    grad_out = noise(seeds[5], (SEQS, LENGTH, DOUT), 1.0, 6.0, ((0, 2), (1, 4)))
    return dict(queries=queries, keys=keys, values=values, log_decay=log_decay, w_out=w_out, grad_out=grad_out)


def block_weights(cumul):
    width = cumul.shape[-1]
    places = jnp.arange(width)
    lower = places[:, None] >= places[None, :]
    spread = cumul[..., :, None] - cumul[..., None, :]
    return jnp.exp(jnp.where(lower, spread, -jnp.inf))


def to_blocks(array, block_total):
    return array.reshape(block_total, BLOCK, H, DH).transpose(0, 2, 1, 3)


def from_blocks(array, block_total):
    return array.transpose(0, 2, 1, 3).reshape(block_total * BLOCK, H * DH)


def reference(queries, keys, values, log_decay, w_out, grad_out):
    scale = 1.0 / DH
    block_total = LENGTH // BLOCK
    panel = w_out.astype(jnp.float32)
    w_grad = jnp.zeros((DH, H, DOUT), jnp.float32)
    mixed_list = []
    qgrad_list = []
    kgrad_list = []
    vgrad_list = []
    for sequence in range(SEQS):
        query_blocks = to_blocks(queries[sequence], block_total)
        key_blocks = to_blocks(keys[sequence], block_total)
        value_blocks = to_blocks(values[sequence], block_total)
        cumul = jnp.cumsum(log_decay[sequence].reshape(H, block_total, BLOCK).transpose(1, 0, 2), axis=-1)

        def forward_step(state, inputs):
            query_here, key_here, value_here, cumul_here = inputs
            weights = block_weights(cumul_here)
            scores = jnp.einsum('htd,hjd->htj', query_here.astype(jnp.float32), key_here.astype(jnp.float32))
            probs = (scores * scale * weights).astype(jnp.bfloat16)
            state_low = state.astype(jnp.bfloat16)
            decay_multiplier = scale * jnp.exp(cumul_here)
            intra = jnp.einsum('htj,hjd->htd', probs.astype(jnp.float32), value_here.astype(jnp.float32))
            inter = jnp.einsum('htd,hde->hte', query_here.astype(jnp.float32), state_low.astype(jnp.float32))
            attended = (intra + inter * decay_multiplier[:, :, None]).astype(jnp.bfloat16)
            tail = jnp.exp(cumul_here[:, -1:] - cumul_here)
            keys_weighted = (key_here.astype(jnp.float32) * tail[:, :, None]).astype(jnp.bfloat16)
            contrib = jnp.einsum('htd,hte->hde', keys_weighted.astype(jnp.float32), value_here.astype(jnp.float32))
            new_state = jnp.exp(cumul_here[:, -1])[:, None, None] * state + contrib
            return new_state, (attended, state_low)

        start_state = jnp.zeros((H, DH, DH), jnp.float32)
        _, (attended_blocks, state_blocks) = lax.scan(forward_step, start_state, (query_blocks, key_blocks, value_blocks, cumul))
        attended_row_list = from_blocks(attended_blocks, block_total).reshape(LENGTH, H, DH)
        cotangent = grad_out[sequence].astype(jnp.float32)
        mixed = jnp.einsum('thd,dho->to', attended_row_list.astype(jnp.float32), panel).astype(jnp.bfloat16)
        grad_heads = jnp.einsum('to,dho->thd', cotangent, panel).astype(jnp.bfloat16)
        w_grad = w_grad + jnp.einsum('thd,to->dho', attended_row_list.astype(jnp.float32), cotangent)
        grad_blocks = to_blocks(grad_heads.reshape(LENGTH, H * DH), block_total)

        def backward_step(back_state, inputs):
            query_here, key_here, value_here, grad_here, cumul_here, state_low = inputs
            weights = block_weights(cumul_here)
            query_f = query_here.astype(jnp.float32)
            key_f = key_here.astype(jnp.float32)
            value_f = value_here.astype(jnp.float32)
            grad_f = grad_here.astype(jnp.float32)
            scores = jnp.einsum('htd,hjd->htj', query_f, key_f)
            probs = (scores * scale * weights).astype(jnp.bfloat16)
            logit_gradient = jnp.einsum('hte,hje->htj', grad_f, value_f)
            dprobs = (logit_gradient * scale * weights).astype(jnp.bfloat16)
            back_low = back_state.astype(jnp.bfloat16)
            decay_multiplier = scale * jnp.exp(cumul_here)
            tail = jnp.exp(cumul_here[:, -1:] - cumul_here)
            dprobs_f = dprobs.astype(jnp.float32)
            back_f = back_low.astype(jnp.float32)
            query_grad = jnp.einsum('htj,hjd->htd', dprobs_f, key_f) + jnp.einsum('hte,hde->htd', grad_f, state_low.astype(jnp.float32)) * decay_multiplier[:, :, None]
            key_grad = jnp.einsum('htj,htd->hjd', dprobs_f, query_f) + tail[:, :, None] * jnp.einsum('hje,hde->hjd', value_f, back_f)
            value_grad = jnp.einsum('htj,hte->hje', probs.astype(jnp.float32), grad_f) + tail[:, :, None] * jnp.einsum('hjd,hde->hje', key_f, back_f)
            queries_weighted = (query_f * decay_multiplier[:, :, None]).astype(jnp.bfloat16)
            earlier = jnp.exp(cumul_here[:, -1])[:, None, None] * back_state + jnp.einsum('htd,hte->hde', queries_weighted.astype(jnp.float32), grad_f)
            return earlier, (query_grad.astype(jnp.bfloat16), key_grad.astype(jnp.bfloat16), value_grad.astype(jnp.bfloat16))

        end_state = jnp.zeros((H, DH, DH), jnp.float32)
        _, (qgrad_blocks, kgrad_blocks, vgrad_blocks) = lax.scan(backward_step, end_state, (query_blocks, key_blocks, value_blocks, grad_blocks, cumul, state_blocks), reverse=True)
        mixed_list.append(mixed)
        qgrad_list.append(from_blocks(qgrad_blocks, block_total))
        kgrad_list.append(from_blocks(kgrad_blocks, block_total))
        vgrad_list.append(from_blocks(vgrad_blocks, block_total))
    return (jnp.stack(mixed_list), jnp.stack(qgrad_list), jnp.stack(kgrad_list), jnp.stack(vgrad_list), w_grad)
```

```python
import functools

import jax
import jax.numpy as jnp
from jax import lax
from jax.experimental import pallas as pl
from jax.experimental.pallas import tpu as pltpu
from jax.sharding import PartitionSpec as P

DH = 128
SCALE = 1.0 / DH
F32 = jnp.float32
BF16 = jnp.bfloat16
EXTRA = 16


def contract(a, b, dim_a, dim_b):
    return lax.dot_general(a, b, (((dim_a,), (dim_b,)), ((), ())), preferred_element_type=F32)


def head(ref, h):
    return ref[:, h * DH : (h + 1) * DH]


def call(kernel, out_shape, scratch=()):
    return pl.pallas_call(
        kernel,
        out_shape=out_shape,
        scratch_shapes=list(scratch),
        compiler_params=pltpu.CompilerParams(vmem_limit_bytes=48 * 1024 * 1024),
    )


def struct(shape, dtype):
    return jax.ShapeDtypeStruct(shape, dtype)


def store_decay(out_ref, row, groups):
    decay = jnp.broadcast_to(jnp.exp(row[:, -1:]), (groups, DH))
    high = decay.astype(BF16).astype(F32)
    both = jnp.concatenate([high, decay - high], axis=0)
    out_ref[groups * DH : groups * DH + EXTRA, :] = both.astype(BF16)


def load_decay(ref, groups):
    both = ref[groups * DH : groups * DH + EXTRA, :].astype(F32)
    return both[:groups] + both[groups:]


def joined(refs, decays, h):
    total = refs[-1][h * DH : (h + 1) * DH, :].astype(F32)
    for ref, decay in zip(refs[-2::-1], decays[::-1]):
        total = ref[h * DH : (h + 1) * DH, :].astype(F32) + decay[h : h + 1, :] * total
    return total


def lower_mask(size):
    return lax.broadcasted_iota(jnp.int32, (size, size), 0) >= lax.broadcasted_iota(
        jnp.int32, (size, size), 1
    )


def contrib_kernel(groups, k_ref, v_ref, ld_ref, state_ref, row_ref, col_ref):
    size = k_ref.shape[0]
    lower = lower_mask(size).astype(F32)
    ld = ld_ref[...]
    row = lax.dot_general(
        ld, lower, (((1,), (1,)), ((), ())), precision=lax.Precision.HIGHEST, preferred_element_type=F32
    )
    col = lax.dot_general(
        lower, ld, (((1,), (1,)), ((), ())), precision=lax.Precision.HIGHEST, preferred_element_type=F32
    )
    row_ref[...] = row
    col_ref[...] = col
    tail = jnp.exp(col[size - 1 :, :] - col)
    for h in range(groups):
        weighted = (head(k_ref, h).astype(F32) * tail[:, h : h + 1]).astype(BF16)
        state_ref[h * DH : (h + 1) * DH, :] = contract(weighted, head(v_ref, h), 0, 0).astype(BF16)
    store_decay(state_ref, row, groups)


def spread_weights(row_ref, col_ref, lower, h):
    spread = col_ref[:, h : h + 1] - row_ref[h : h + 1, :]
    return jnp.exp(jnp.where(lower, spread, -jnp.inf))


def intra_kernel(groups, q_ref, k_ref, v_ref, row_ref, col_ref, probs_ref, intra_ref):
    lower = lower_mask(q_ref.shape[0])
    for h in range(groups):
        weights = spread_weights(row_ref, col_ref, lower, h)
        probs = (contract(head(q_ref, h), head(k_ref, h), 1, 1) * SCALE * weights).astype(BF16)
        probs_ref[h] = probs
        intra_ref[:, h * DH : (h + 1) * DH] = contract(probs, head(v_ref, h), 1, 0)


def attended_kernel(groups, count, *refs):
    states = refs[:count]
    q_ref, intra_ref, col_ref, pick_own_ref, pick_other_ref = refs[count : count + 5]
    own_ref, other_ref, low_ref, attended_ref = refs[count + 5 :]
    decays = [load_decay(ref, groups) for ref in states[:-1]]
    factor = jnp.exp(col_ref[...]) * SCALE
    for h in range(groups):
        low = joined(states, decays, h).astype(BF16)
        low_ref[h] = low
        inter = contract(head(q_ref, h), low, 1, 0)
        attended_ref[:, h * DH : (h + 1) * DH] = (
            head(intra_ref, h) + inter * factor[:, h : h + 1]
        ).astype(BF16)
    own_ref[...] = contract(attended_ref[...], pick_own_ref[...], 1, 0).astype(BF16)
    other_ref[...] = contract(attended_ref[...], pick_other_ref[...], 1, 0).astype(BF16)


def back_contrib_kernel(
    groups, own_ref, other_ref, pick_own_ref, pick_other_ref, q_ref, row_ref, col_ref, grad_ref, state_ref
):
    grad_ref[...] = (
        contract(own_ref[...], pick_own_ref[...], 1, 1) + contract(other_ref[...], pick_other_ref[...], 1, 1)
    ).astype(BF16)
    factor = jnp.exp(col_ref[...]) * SCALE
    for h in range(groups):
        weighted = (head(q_ref, h).astype(F32) * factor[:, h : h + 1]).astype(BF16)
        state_ref[h * DH : (h + 1) * DH, :] = contract(weighted, head(grad_ref, h), 0, 0).astype(BF16)
    store_decay(state_ref, row_ref[...], groups)


def back_intra_kernel(
    groups, grad_ref, q_ref, k_ref, v_ref, row_ref, col_ref, probs_ref, low_ref, qgrad_ref, kpart_ref, vpart_ref
):
    lower = lower_mask(q_ref.shape[0])
    factor = jnp.exp(col_ref[...]) * SCALE
    for h in range(groups):
        here = slice(h * DH, (h + 1) * DH)
        grad = head(grad_ref, h)
        weights = spread_weights(row_ref, col_ref, lower, h)
        dprobs = (contract(grad, head(v_ref, h), 1, 1) * SCALE * weights).astype(BF16)
        qgrad_ref[:, here] = (
            contract(dprobs, head(k_ref, h), 1, 0) + contract(grad, low_ref[h], 1, 1) * factor[:, h : h + 1]
        ).astype(BF16)
        kpart_ref[:, here] = contract(dprobs, head(q_ref, h), 0, 0)
        vpart_ref[:, here] = contract(probs_ref[h], grad, 0, 0)


def back_inter_kernel(groups, count, *refs):
    states = refs[:count]
    k_ref, v_ref, col_ref, kpart_ref, vpart_ref, kgrad_ref, vgrad_ref = refs[count:]
    decays = [load_decay(ref, groups) for ref in states[:-1]]
    col = col_ref[...]
    tail = jnp.exp(col[col.shape[0] - 1 :, :] - col)
    for h in range(groups):
        here = slice(h * DH, (h + 1) * DH)
        low = joined(states, decays, h).astype(BF16)
        kgrad_ref[:, here] = (
            head(kpart_ref, h) + tail[:, h : h + 1] * contract(head(v_ref, h), low, 1, 1)
        ).astype(BF16)
        vgrad_ref[:, here] = (
            head(vpart_ref, h) + tail[:, h : h + 1] * contract(head(k_ref, h), low, 1, 0)
        ).astype(BF16)


def neighbours(state, devices, forward):
    out = []
    for hop in range(1, devices):
        if forward:
            pairs = [(i, i + hop) for i in range(devices - hop)]
        else:
            pairs = [(i + hop, i) for i in range(devices - hop)]
        out.append(lax.ppermute(state, "ctx", pairs))
    return out


def swapped(array):
    return lax.ppermute(array, "dp", [(0, 1), (1, 0)])


def flipped(array, bit):
    return lax.ppermute(array, "ctx", [(i, i ^ bit) for i in range(4)])


def gather_rows(w):
    if lax.axis_size("ctx") != 4:
        return lax.all_gather(w, "ctx", axis=0, tiled=True)
    half = w.shape[1] // 2
    one, two = flipped(w, 1), flipped(w, 2)
    three = jnp.concatenate([flipped(one[:, :half], 2), flipped(two[:, half:], 1)], axis=1)
    return jnp.concatenate([w, one, two, three], axis=0)


def scatter_rows(attended, cotangent):
    devices = lax.axis_size("ctx")
    if devices != 4:
        part = contract(attended, cotangent, 0, 0).astype(BF16)
        return lax.psum_scatter(part, "ctx", scatter_dimension=0, tiled=True).astype(F32)
    rows = attended.shape[1] // devices
    half = cotangent.shape[1] // 2
    left, right = cotangent[:, :half], cotangent[:, half:]

    def part(k, columns):
        return contract(attended[:, k * rows : (k + 1) * rows], columns, 0, 0)

    far_left = flipped(part(3, left).astype(BF16), 1)
    far_right = flipped(part(3, right).astype(BF16), 2)
    near_left = flipped(part(1, left).astype(BF16), 1)
    near_right = flipped(part(2, right).astype(BF16), 2)
    on_left = flipped((part(2, left) + far_left.astype(F32)).astype(BF16), 2)
    on_right = flipped((part(1, right) + far_right.astype(F32)).astype(BF16), 1)
    return jnp.concatenate(
        [
            part(0, left) + near_left.astype(F32) + on_left.astype(F32),
            part(0, right) + near_right.astype(F32) + on_right.astype(F32),
        ],
        axis=1,
    )


def ring_scatter(own, other):
    devices, mine = lax.axis_size("head"), lax.axis_index("head")
    width = own.shape[1] // devices
    around = [(i, (i + 1) % devices) for i in range(devices)]

    def columns(array, k):
        start = lax.rem(mine - k + devices, devices) * width
        return lax.dynamic_slice_in_dim(array, start, width, axis=1)

    total = None
    for k in range(1, devices + 1):
        here = columns(own, k).astype(F32) + swapped(columns(other, k).astype(BF16)).astype(F32)
        if total is not None:
            here = here + lax.ppermute(total, "head", around).astype(F32)
        total = here.astype(BF16)
    return total


def picks(groups, rows_each):
    devices, mine, core = lax.axis_size("ctx"), lax.axis_index("ctx"), lax.axis_index("dp")
    width = devices * rows_each * groups
    feature = lax.broadcasted_iota(jnp.int32, (groups * DH, width), 0)
    place = lax.broadcasted_iota(jnp.int32, (groups * DH, width), 1)
    block = place // (rows_each * groups)
    if devices == 4:
        block = block ^ mine
    row = (place // groups) % rows_each
    group = place % groups

    def pick(p):
        return (feature == group * DH + (block * 2 + p) * rows_each + row).astype(BF16)

    return pick(core), pick(1 - core)


def shards(queries, keys, values, log_decay, w_out, grad_out):
    groups = log_decay.shape[1]
    size = queries.shape[1]
    devices = lax.axis_size("ctx")
    q, k, v, ld, g = queries[0], keys[0], values[0], log_decay[0], grad_out[0]
    rows_each, _, width = w_out.shape
    w = w_out.reshape(rows_each * groups, width)
    features = groups * DH
    state_shape = struct((features + EXTRA, DH), BF16)
    flat = lambda dtype: struct((size, features), dtype)
    half = struct((size, features // 2), BF16)

    w_all = gather_rows(w)
    g_all = jnp.concatenate([g, swapped(g)], axis=0)

    state, row, col = call(
        functools.partial(contrib_kernel, groups),
        (state_shape, struct((groups, size), F32), struct((size, groups), F32)),
    )(k, v, ld)
    before = neighbours(state, devices, True)
    pick_own, pick_other = picks(groups, rows_each)
    probs, intra = call(
        functools.partial(intra_kernel, groups), (struct((groups, size, size), BF16), flat(F32))
    )(q, k, v, row, col)
    a_own, a_other, low = call(
        functools.partial(attended_kernel, groups, len(before)),
        (half, half, struct((groups, DH, DH), BF16)),
        [pltpu.VMEM((size, features), BF16)],
    )(*before, q, intra, col, pick_own, pick_other)
    a_all = jnp.concatenate([a_own, swapped(a_other)], axis=0)

    w_grad = scatter_rows(a_all, g_all)
    grad_heads = contract(g_all, w_all, 1, 1).astype(BF16)
    grad_other = swapped(grad_heads[size:])
    grad, back = call(
        functools.partial(back_contrib_kernel, groups), (flat(BF16), state_shape)
    )(grad_heads[:size], grad_other, pick_own, pick_other, q, row, col)
    after = neighbours(back, devices, False)

    partial_out = contract(a_all, w_all, 1, 0)
    mixed = ring_scatter(partial_out[:size], partial_out[size:])

    query_grad, key_part, value_part = call(
        functools.partial(back_intra_kernel, groups), (flat(BF16), flat(F32), flat(F32))
    )(grad, q, k, v, row, col, probs, low)
    key_grad, value_grad = call(
        functools.partial(back_inter_kernel, groups, len(after)), (flat(BF16), flat(BF16))
    )(*after, k, v, col, key_part, value_part)
    return (
        mixed[None],
        query_grad[None],
        key_grad[None],
        value_grad[None],
        w_grad.reshape(rows_each, groups, width),
    )


def solution(mesh):
    return jax.shard_map(
        shards,
        mesh=mesh,
        in_specs=(
            P("dp", "ctx", "head"),
            P("dp", "ctx", "head"),
            P("dp", "ctx", "head"),
            P("dp", "head", "ctx"),
            P(("ctx", "dp"), "head", None),
            P("dp", "ctx", None),
        ),
        out_specs=(
            P("dp", "ctx", "head"),
            P("dp", "ctx", "head"),
            P("dp", "ctx", "head"),
            P("dp", "ctx", "head"),
            P(("ctx", "dp"), "head", None),
        ),
        check_vma=False,
    )
```

```python
import functools

import jax
import jax.numpy as jnp
from jax import lax
from jax.experimental import pallas as pl
from jax.experimental.pallas import tpu as pltpu
from jax.sharding import PartitionSpec as P

DH = 128
SCALE = 1.0 / DH
F32 = jnp.float32
BF16 = jnp.bfloat16
EXTRA = 16


def contract(a, b, dim_a, dim_b):
    return lax.dot_general(a, b, (((dim_a,), (dim_b,)), ((), ())), preferred_element_type=F32)


def head(ref, h):
    return ref[:, h * DH : (h + 1) * DH]


def call(kernel, out_shape, *args, staged=(), free_in=(), free_out=(), scratch=(), after=(), room=24):
    n, waits, count = len(args), len(after), len(staged)

    def body(*refs):
        ins, rest = list(refs[:n]), refs[n + waits :]
        rest, buffers, sem = rest[: len(rest) - count - 1], rest[len(rest) - count - 1 : -1], rest[-1]
        copies = [pltpu.make_async_copy(ins[i], buffers[j], sem.at[j]) for j, i in enumerate(staged)]
        for copy in copies:
            copy.start()
        for copy in copies:
            copy.wait()
        for j, i in enumerate(staged):
            ins[i] = buffers[j]
        kernel(*ins, *rest)

    anywhere, local, far = (pl.BlockSpec(memory_space=m) for m in (pl.ANY, pltpu.VMEM, pltpu.HBM))
    specs = [far if i in free_out else local for i in range(len(jax.tree.leaves(out_shape)))]
    return pl.pallas_call(
        body,
        out_shape=out_shape,
        in_specs=[far if i in staged or i in free_in else local for i in range(n)] + [anywhere] * waits,
        out_specs=specs if isinstance(out_shape, (list, tuple)) else specs[0],
        scratch_shapes=[
            *scratch,
            *[pltpu.VMEM(args[i].shape, args[i].dtype) for i in staged],
            pltpu.SemaphoreType.DMA((max(count, 1),)),
        ],
        compiler_params=pltpu.CompilerParams(vmem_limit_bytes=room * 1024 * 1024),
        cost_estimate=pl.CostEstimate(flops=0, bytes_accessed=0, transcendentals=0),
    )(*args, *after)


def struct(shape, dtype):
    return jax.ShapeDtypeStruct(shape, dtype)


def store_decay(out_ref, row, groups):
    decay = jnp.broadcast_to(jnp.exp(row[:, -1:]), (groups, DH))
    high = decay.astype(BF16).astype(F32)
    both = jnp.concatenate([high, decay - high], axis=0)
    out_ref[groups * DH : groups * DH + EXTRA, :] = both.astype(BF16)


def load_decay(ref, groups):
    both = ref[groups * DH : groups * DH + EXTRA, :].astype(F32)
    return both[:groups] + both[groups:]


def entering(refs, groups, forward):
    if lax.axis_size("ctx") == 4:
        near, far = refs
        bit = side(forward)
        decay = load_decay(near, groups) * bit + (1.0 - bit)
        return lambda h: rows_of(near, h) * bit + decay[h : h + 1, :] * rows_of(far, h)
    decays = [load_decay(ref, groups) for ref in refs[:-1]]

    def state(h):
        total = rows_of(refs[-1], h)
        for ref, decay in zip(refs[-2::-1], decays[::-1]):
            total = rows_of(ref, h) + decay[h : h + 1, :] * total
        return total

    return state


def rows_of(ref, h):
    return ref[h * DH : (h + 1) * DH, :].astype(F32)


def side(forward):
    bit = lax.rem(lax.axis_index("ctx"), 2).astype(F32)
    return bit if forward else 1.0 - bit


def pair_kernel(groups, forward, own_ref, near_ref, *refs):
    out_ref = refs[-1]
    if len(refs) == 3:
        refs[1][...] = refs[0][...]
    bit = side(forward)
    own_decay, near_decay = load_decay(own_ref, groups), load_decay(near_ref, groups)
    for h in range(groups):
        here = slice(h, h + 1)
        own, near = rows_of(own_ref, h), rows_of(near_ref, h)
        own_share = bit + (1.0 - bit) * near_decay[here]
        near_share = bit * own_decay[here] + (1.0 - bit)
        out_ref[h * DH : (h + 1) * DH, :] = (own_share * own + near_share * near).astype(BF16)


def lower_mask(size):
    return lax.broadcasted_iota(jnp.int32, (size, size), 0) >= lax.broadcasted_iota(
        jnp.int32, (size, size), 1
    )


def ring_columns(w_ref, out_ref, hops, sem):
    width = w_ref.shape[1] // lax.axis_size("head")
    copies = []
    for j in range(out_ref.shape[1] // width):
        here = pl.ds(j * width, width)
        copies.append(pltpu.make_async_copy(w_ref.at[:, columns_after(hops + j, width)], out_ref.at[:, here], sem.at[j]))
        copies[-1].start()
    return copies


def first_columns_kernel(w_ref, out_ref, sem):
    for copy in ring_columns(w_ref, out_ref, 1, sem):
        copy.wait()


def contrib_kernel(groups, hops, k_ref, v_ref, ld_ref, w_ref, state_ref, row_ref, col_ref, copy_ref, sem):
    copies = ring_columns(w_ref, copy_ref, hops, sem)
    size = k_ref.shape[0]
    lower = lower_mask(size).astype(F32)
    ld = ld_ref[...]
    row = lax.dot_general(
        ld, lower, (((1,), (1,)), ((), ())), precision=lax.Precision.HIGHEST, preferred_element_type=F32
    )
    col = lax.dot_general(
        lower, ld, (((1,), (1,)), ((), ())), precision=lax.Precision.HIGHEST, preferred_element_type=F32
    )
    row_ref[...] = row
    col_ref[...] = col
    tail = jnp.exp(col[size - 1 :, :] - col)
    for h in range(groups):
        weighted = (head(k_ref, h).astype(F32) * tail[:, h : h + 1]).astype(BF16)
        state_ref[h * DH : (h + 1) * DH, :] = contract(weighted, head(v_ref, h), 0, 0).astype(BF16)
    store_decay(state_ref, row, groups)
    for copy in copies:
        copy.wait()


def spread_weights(row_ref, col_ref, lower, h):
    spread = col_ref[:, h : h + 1] - row_ref[h : h + 1, :]
    return jnp.exp(jnp.where(lower, spread, -jnp.inf))


def intra_kernel(groups, q_ref, k_ref, v_ref, row_ref, col_ref, probs_ref, intra_ref):
    lower = lower_mask(q_ref.shape[0])
    for h in range(groups):
        weights = spread_weights(row_ref, col_ref, lower, h)
        probs = (contract(head(q_ref, h), head(k_ref, h), 1, 1) * SCALE * weights).astype(BF16)
        probs_ref[h] = probs
        intra_ref[:, h * DH : (h + 1) * DH] = contract(probs, head(v_ref, h), 1, 0)


def attended_kernel(groups, count, *refs):
    states = refs[:count]
    q_ref, intra_ref, col_ref, pick_own_ref, pick_other_ref = refs[count : count + 5]
    own_ref, other_ref, low_ref, attended_ref = refs[count + 5 :]
    state = entering(states, groups, True)
    factor = jnp.exp(col_ref[...]) * SCALE
    for h in range(groups):
        low = state(h).astype(BF16)
        low_ref[h] = low
        inter = contract(head(q_ref, h), low, 1, 0)
        attended_ref[:, h * DH : (h + 1) * DH] = (
            head(intra_ref, h) + inter * factor[:, h : h + 1]
        ).astype(BF16)
    own_ref[...] = contract(attended_ref[...], pick_own_ref[...], 1, 0).astype(BF16)
    other_ref[...] = contract(attended_ref[...], pick_other_ref[...], 1, 0).astype(BF16)


def back_contrib_kernel(
    groups, own_ref, other_ref, pick_own_ref, pick_other_ref, q_ref, row_ref, col_ref, grad_ref, state_ref
):
    grad_ref[...] = (
        contract(own_ref[...], pick_own_ref[...], 1, 1) + contract(other_ref[...], pick_other_ref[...], 1, 1)
    ).astype(BF16)
    factor = jnp.exp(col_ref[...]) * SCALE
    for h in range(groups):
        weighted = (head(q_ref, h).astype(F32) * factor[:, h : h + 1]).astype(BF16)
        state_ref[h * DH : (h + 1) * DH, :] = contract(weighted, head(grad_ref, h), 0, 0).astype(BF16)
    store_decay(state_ref, row_ref[...], groups)


def back_intra_kernel(
    groups, grad_ref, q_ref, k_ref, v_ref, row_ref, col_ref, probs_ref, low_ref, qgrad_ref, kpart_ref, vpart_ref
):
    lower = lower_mask(q_ref.shape[0])
    factor = jnp.exp(col_ref[...]) * SCALE
    for h in range(groups):
        here = slice(h * DH, (h + 1) * DH)
        grad = head(grad_ref, h)
        weights = spread_weights(row_ref, col_ref, lower, h)
        dprobs = (contract(grad, head(v_ref, h), 1, 1) * SCALE * weights).astype(BF16)
        qgrad_ref[:, here] = (
            contract(dprobs, head(k_ref, h), 1, 0) + contract(grad, low_ref[h], 1, 1) * factor[:, h : h + 1]
        ).astype(BF16)
        kpart_ref[:, here] = contract(dprobs, head(q_ref, h), 0, 0)
        vpart_ref[:, here] = contract(probs_ref[h], grad, 0, 0)


def back_inter_kernel(groups, count, *refs):
    states = refs[:count]
    k_ref, v_ref, col_ref, kpart_ref, vpart_ref, kgrad_ref, vgrad_ref = refs[count:]
    state = entering(states, groups, False)
    col = col_ref[...]
    tail = jnp.exp(col[col.shape[0] - 1 :, :] - col)
    for h in range(groups):
        here = slice(h * DH, (h + 1) * DH)
        low = state(h).astype(BF16)
        kgrad_ref[:, here] = (
            head(kpart_ref, h) + tail[:, h : h + 1] * contract(head(v_ref, h), low, 1, 1)
        ).astype(BF16)
        vgrad_ref[:, here] = (
            head(vpart_ref, h) + tail[:, h : h + 1] * contract(head(k_ref, h), low, 1, 0)
        ).astype(BF16)


def hops_of(state, forward):
    devices = lax.axis_size("ctx")
    out = []
    for hop in range(1, devices):
        if forward:
            pairs = [(i, i + hop) for i in range(devices - hop)]
        else:
            pairs = [(i + hop, i) for i in range(devices - hop)]
        out.append(lax.ppermute(state, "ctx", pairs))
    return out


def swapped(array):
    return lax.ppermute(array, "dp", [(0, 1), (1, 0)])


def flipped(array, bit):
    return lax.ppermute(array, "ctx", [(i, i ^ bit) for i in range(4)])


def rows_kernel(count, *refs):
    ins, outs = refs[: len(refs) // 2], refs[len(refs) // 2 :]
    for i, (ref, out) in enumerate(zip(ins, outs)):
        rows = out.shape[0]
        out[...] = ref[:rows] if i < count else ref[rows:]


def lay_out(pieces, out_ref, columns=slice(None)):
    top = 0
    for piece in pieces:
        out_ref[top : top + piece.shape[0], :] = piece[:, columns]
        top += piece.shape[0]


def columns_after(hops, width):
    devices = lax.axis_size("head")
    return pl.ds(pl.multiple_of(lax.rem(lax.axis_index("head") + hops, devices) * width, width), width)


def mix_kernel(count, place, a_own, a_other, *refs):
    pieces, owns, other, w_ref = refs[:count], refs[count:-2], refs[-2], refs[-1]
    width = w_ref.shape[1]
    for j, own in enumerate(owns):
        lay_out(pieces, w_ref, slice((place + j) * width, (place + j + 1) * width))
        own[...] = contract(a_own[...], w_ref[...], 1, 0)
        other[:, j * width : (j + 1) * width] = contract(a_other[...], w_ref[...], 1, 0).astype(BF16)


def grad_kernel(count, g_own, g_other, *refs):
    first, rest, (own, other, w_ref) = refs[:count], refs[count : 2 * count], refs[2 * count :]
    heads = lax.axis_size("head")
    left, width = first[0].shape[1], w_ref.shape[1] // heads
    lay_out(first, w_ref.at[:, 0:left])
    lay_out(rest, w_ref.at[:, left:])
    for g_ref, out in ((g_own, own), (g_other, other)):
        total = None
        for j in range(heads):
            term = contract(
                g_ref[:, columns_after(1 + j, width)], w_ref[:, j * width : (j + 1) * width], 1, 1
            )
            total = term if total is None else total + term
        out[...] = total.astype(BF16)


def weight_kernel(blocks, a_own, a_other, g_own, g_other, *outs):
    rows = a_own.shape[1] // 4
    for (k, left, right), out in zip(blocks, outs):
        here = slice(k * rows, (k + 1) * rows)
        out[...] = (
            contract(a_own[:, here], g_own[:, left:right], 0, 0)
            + contract(a_other[:, here], g_other[:, left:right], 0, 0)
        ).astype(out.dtype)


def onward_kernel(mid_left, mid_right, far_left, far_right, left_ref, right_ref):
    left_ref[...] = (mid_left[...] + far_left[...].astype(F32)).astype(BF16)
    right_ref[...] = (mid_right[...] + far_right[...].astype(F32)).astype(BF16)


def total_kernel(own_ref, left_ref, right_ref, out_ref):
    half = own_ref.shape[1] // 2
    left, right = slice(0, half), slice(half, 2 * half)
    out_ref[:, left] = own_ref[:, left] + left_ref[...].astype(F32)
    out_ref[:, right] = own_ref[:, right] + right_ref[...].astype(F32)


def ring_kernel(j, own_ref, other_ref, *refs):
    width = own_ref.shape[1]
    total = own_ref[...] + other_ref[:, j * width : (j + 1) * width].astype(F32)
    if len(refs) == 2:
        total = total + refs[0][...].astype(F32)
    refs[-1][...] = total.astype(BF16)


def passed(array):
    devices = lax.axis_size("head")
    return lax.ppermute(array, "head", [(i, (i - 1) % devices) for i in range(devices)])


def picks(groups, rows_each):
    devices, mine, core = lax.axis_size("ctx"), lax.axis_index("ctx"), lax.axis_index("dp")
    width = devices * rows_each * groups
    feature = lax.broadcasted_iota(jnp.int32, (groups * DH, width), 0)
    place = lax.broadcasted_iota(jnp.int32, (groups * DH, width), 1)
    block = place // (rows_each * groups)
    if devices == 4:
        block = block ^ mine
    row = (place // groups) % rows_each
    group = place % groups

    def pick(p):
        return (feature == group * DH + (block * 2 + p) * rows_each + row).astype(BF16)

    return pick(core), pick(1 - core)


def shards(queries, keys, values, log_decay, w_out, grad_out):
    groups = log_decay.shape[1]
    size = queries.shape[1]
    devices, heads = lax.axis_size("ctx"), lax.axis_size("head")
    four = devices == 4
    q, k, v, ld, g = queries[0], keys[0], values[0], log_decay[0], grad_out[0]
    rows_each, _, width = w_out.shape
    rows, part, middle = rows_each * groups, width // heads, width // 2
    w = w_out.reshape(rows, width)
    features = groups * DH
    state_shape = struct((features + EXTRA, DH), BF16)
    flat = lambda dtype: struct((size, features), dtype)
    half = struct((size, features // 2), BF16)
    last = []

    def step(kernel, out_shape, *args, after=(), **kwargs):
        out = call(kernel, out_shape, *args, after=[*last, *after], **kwargs)
        last[:] = [min(jax.tree.leaves(out), key=lambda x: x.size)]
        return out

    near_heads = heads // 2
    w_first = step(
        first_columns_kernel,
        struct((rows, near_heads * part), BF16),
        w,
        free_in=(0,),
        scratch=[pltpu.SemaphoreType.DMA((near_heads,))],
        room=60,
    )
    if four:
        first_two, first_one = flipped(w_first, 2), flipped(w_first, 1)
    g_other = swapped(g)
    rest_shape = struct((rows, width - near_heads * part), BF16)
    state, row, col, w_rest = step(
        functools.partial(contrib_kernel, groups, near_heads + 1),
        (state_shape, struct((groups, size), F32), struct((size, groups), F32), rest_shape),
        k,
        v,
        ld,
        w,
        staged=(0, 1, 2),
        free_in=(3,),
        scratch=[pltpu.SemaphoreType.DMA((heads - near_heads,))],
        room=60,
    )
    if four:
        near = flipped(state, 1)
        rest_two = flipped(w_rest, 2)
    else:
        before = hops_of(state, True)
    pick_own, pick_other = picks(groups, rows_each)
    probs, intra = step(
        functools.partial(intra_kernel, groups),
        (struct((groups, size, size), BF16), flat(F32)),
        q,
        k,
        v,
        row,
        col,
        staged=(0, 1, 2),
        after=[g_other],
    )
    if four:
        lower = lambda array: struct((rows // 2, array.shape[1]), BF16)
        on_one, on_two = step(
            functools.partial(rows_kernel, 1), [lower(w_first)] * 2, first_one, first_two
        )
        first = [w_first, first_one, first_two, flipped(on_one, 2), flipped(on_two, 1)]
        w_again, pair = step(
            functools.partial(pair_kernel, groups, True), [rest_shape, struct((features, DH), BF16)], state, near, w_rest
        )
        before = [near, lax.ppermute(pair, "ctx", [(0, 2), (1, 3)])]
        rest_one = flipped(w_again, 1)
        (on_two,) = step(functools.partial(rows_kernel, 0), [lower(w_rest)], rest_two, after=first[3:])
    else:
        first = [lax.all_gather(w_first, "ctx", axis=0, tiled=True)]
        rest = [lax.all_gather(w_rest, "ctx", axis=0, tiled=True)]
    a_own, a_away, low = step(
        functools.partial(attended_kernel, groups, len(before)),
        (half, half, struct((groups, DH, DH), BF16)),
        *before,
        q,
        intra,
        col,
        pick_own,
        pick_other,
        staged=(len(before),),
        scratch=[pltpu.VMEM((size, features), BF16)],
    )
    a_other = swapped(a_away)
    if four:
        (on_one,) = step(functools.partial(rows_kernel, 1), [lower(w_rest)], rest_one)
        rest = [w_rest, rest_one, rest_two, flipped(on_one, 2), flipped(on_two, 1)]

    held = pltpu.VMEM((features // 2, part), BF16)

    def mix(pieces, place, count):
        out = step(
            functools.partial(mix_kernel, len(pieces), place),
            [struct((size, part), F32)] * count + [struct((size, count * part), BF16)],
            a_own,
            a_other,
            *pieces,
            scratch=[held],
        )
        away = swapped(out[-1])
        return [(own, away, j) for j, own in enumerate(out[:-1])]

    def ring(terms, *arrived):
        own, away, j = terms
        return step(functools.partial(ring_kernel, j), struct((size, part), BF16), own, away, *arrived)

    def weights(blocks, shapes):
        return step(functools.partial(weight_kernel, blocks), shapes, a_own, a_other, g, g_other, staged=(2,))

    def grad_of(some):
        here = sum(piece.shape[0] for piece, _ in some)
        return step(
            functools.partial(grad_kernel, len(some)),
            [struct((size, here), BF16)] * 2,
            g,
            g_other,
            *[piece for piece, _ in some],
            *[piece for _, piece in some],
            staged=(0,),
            scratch=[pltpu.VMEM((here, width), BF16)],
        )

    terms = mix(first, 0, near_heads)
    if four:
        small = lambda dtype: struct((rows, middle), dtype)
        far = weights([(3, 0, middle), (3, middle, width)], [small(BF16)] * 2)
        far_left, far_right = flipped(far[0], 1), flipped(far[1], 2)
    arrived = passed(ring(terms[0]))
    both = list(zip(first, rest))
    if four:
        near_grads = grad_of(both[:3])
        parts = weights(
            [(2, 0, middle), (1, middle, width), (1, 0, middle), (2, middle, width), (0, 0, width)],
            [small(F32)] * 2 + [small(BF16)] * 2 + [struct((rows, width), F32)],
        )
        last_grads = grad_of(both[3:])
        grad_own = jnp.concatenate([near_grads[0], last_grads[0]], axis=1)
        grad_away = jnp.concatenate([near_grads[1], last_grads[1]], axis=1)
    else:
        grad_own, grad_away = grad_of(both)
    grad_other = swapped(grad_away)
    grad, back = step(
        functools.partial(back_contrib_kernel, groups),
        (flat(BF16), state_shape),
        grad_own,
        grad_other,
        pick_own,
        pick_other,
        q,
        row,
        col,
    )
    if four:
        near = flipped(back, 1)
        to_left, to_right = step(onward_kernel, [small(BF16)] * 2, parts[0], parts[1], far_left, far_right)
        on_left, on_right = flipped(to_left, 2), flipped(to_right, 1)
    else:
        after = hops_of(back, False)
    for j in range(1, near_heads):
        arrived = passed(ring(terms[j], arrived))
    terms = mix(rest, 0, 1)
    query_grad, key_part, value_part = step(
        functools.partial(back_intra_kernel, groups),
        (flat(BF16), flat(F32), flat(F32)),
        grad,
        q,
        k,
        v,
        row,
        col,
        probs,
        low,
        staged=(1, 2, 3),
    )
    if four:
        pair = step(functools.partial(pair_kernel, groups, False), struct((features, DH), BF16), back, near)
        after = [near, lax.ppermute(pair, "ctx", [(2, 0), (3, 1)])]
        w_sum = step(total_kernel, struct((rows, width), F32), parts[4], on_left, on_right)
        near_left, near_right = flipped(parts[2], 1), flipped(parts[3], 2)
    for j in range(1, heads - near_heads):
        arrived = passed(ring(terms[0], arrived))
        terms = mix(rest, j, 1)
    key_grad, value_grad = step(
        functools.partial(back_inter_kernel, groups, len(after)),
        (flat(BF16), flat(BF16)),
        *after,
        k,
        v,
        col,
        key_part,
        value_part,
    )
    if four:
        w_grad = step(total_kernel, struct((rows, width), F32), w_sum, near_left, near_right)
    else:
        w_grad = contract(a_own, g, 0, 0) + contract(a_other, g_other, 0, 0)
        w_grad = lax.psum_scatter(w_grad.astype(BF16), "ctx", scatter_dimension=0, tiled=True).astype(F32)
    mixed = ring(terms[0], arrived)
    return (
        mixed[None],
        query_grad[None],
        key_grad[None],
        value_grad[None],
        w_grad.reshape(rows_each, groups, width),
    )


def solution(mesh):
    return jax.shard_map(
        shards,
        mesh=mesh,
        in_specs=(
            P("dp", "ctx", "head"),
            P("dp", "ctx", "head"),
            P("dp", "ctx", "head"),
            P("dp", "head", "ctx"),
            P(("ctx", "dp"), "head", None),
            P("dp", "ctx", None),
        ),
        out_specs=(
            P("dp", "ctx", "head"),
            P("dp", "ctx", "head"),
            P("dp", "ctx", "head"),
            P("dp", "ctx", "head"),
            P(("ctx", "dp"), "head", None),
        ),
        check_vma=False,
    )
```

```python
import functools

import jax
import jax.numpy as jnp
from jax import lax
from jax.experimental import pallas as pl
from jax.experimental.pallas import tpu as pltpu
from jax.sharding import PartitionSpec as P

DH = 128
SCALE = 1.0 / DH
F32 = jnp.float32
BF16 = jnp.bfloat16
EXTRA = 16
C17, C20, C24 = 1284000000, 1070000000, 2140000000


def contract(a, b, dim_a, dim_b):
    return lax.dot_general(a, b, (((dim_a,), (dim_b,)), ((), ())), preferred_element_type=F32)


def head(ref, h):
    return ref[:, h * DH : (h + 1) * DH]


def call(kernel, out_shape, *args, staged=(), free_in=(), free_out=(), scratch=(), after=(), room=24, work=0):
    n, waits, count = len(args), len(after), len(staged)

    def body(*refs):
        ins, rest = list(refs[:n]), refs[n + waits :]
        rest, buffers, sem = rest[: len(rest) - count - 1], rest[len(rest) - count - 1 : -1], rest[-1]
        copies = [pltpu.make_async_copy(ins[i], buffers[j], sem.at[j]) for j, i in enumerate(staged)]
        for copy in copies:
            copy.start()
        for copy in copies:
            copy.wait()
        for j, i in enumerate(staged):
            ins[i] = buffers[j]
        kernel(*ins, *rest)

    anywhere, local, far = (pl.BlockSpec(memory_space=m) for m in (pl.ANY, pltpu.VMEM, pltpu.HBM))
    specs = [far if i in free_out else local for i in range(len(jax.tree.leaves(out_shape)))]
    return pl.pallas_call(
        body,
        name=getattr(kernel, "func", kernel).__name__,
        out_shape=out_shape,
        in_specs=[far if i in staged or i in free_in else local for i in range(n)] + [anywhere] * waits,
        out_specs=specs if isinstance(out_shape, (list, tuple)) else specs[0],
        scratch_shapes=[
            *scratch,
            *[pltpu.VMEM(args[i].shape, args[i].dtype) for i in staged],
            pltpu.SemaphoreType.DMA((max(count, 1),)),
        ],
        compiler_params=pltpu.CompilerParams(vmem_limit_bytes=room * 1024 * 1024),
        cost_estimate=pl.CostEstimate(flops=work, bytes_accessed=0, transcendentals=0),
    )(*args, *after)


def struct(shape, dtype):
    return jax.ShapeDtypeStruct(shape, dtype)


def store_decay(out_ref, row, groups):
    decay = jnp.broadcast_to(jnp.exp(row[:, -1:]), (groups, DH))
    high = decay.astype(BF16).astype(F32)
    both = jnp.concatenate([high, decay - high], axis=0)
    out_ref[groups * DH : groups * DH + EXTRA, :] = both.astype(BF16)


def load_decay(ref, groups):
    both = ref[groups * DH : groups * DH + EXTRA, :].astype(F32)
    return both[:groups] + both[groups:]


def entering(refs, groups, forward):
    if lax.axis_size("ctx") == 4:
        near, far = refs
        bit = side(forward)
        decay = load_decay(near, groups) * bit + (1.0 - bit)
        return lambda h: rows_of(near, h) * bit + decay[h : h + 1, :] * rows_of(far, h)
    decays = [load_decay(ref, groups) for ref in refs[:-1]]

    def state(h):
        total = rows_of(refs[-1], h)
        for ref, decay in zip(refs[-2::-1], decays[::-1]):
            total = rows_of(ref, h) + decay[h : h + 1, :] * total
        return total

    return state


def rows_of(ref, h):
    return ref[h * DH : (h + 1) * DH, :].astype(F32)


def side(forward):
    bit = lax.rem(lax.axis_index("ctx"), 2).astype(F32)
    return bit if forward else 1.0 - bit


def pair_kernel(groups, forward, own_ref, near_ref, *refs):
    out_ref = refs[-1]
    if len(refs) == 3:
        refs[1][...] = refs[0][...]
    bit = side(forward)
    own_decay, near_decay = load_decay(own_ref, groups), load_decay(near_ref, groups)
    for h in range(groups):
        here = slice(h, h + 1)
        own, near = rows_of(own_ref, h), rows_of(near_ref, h)
        own_share = bit + (1.0 - bit) * near_decay[here]
        near_share = bit * own_decay[here] + (1.0 - bit)
        out_ref[h * DH : (h + 1) * DH, :] = (own_share * own + near_share * near).astype(BF16)


def lower_mask(size):
    return lax.broadcasted_iota(jnp.int32, (size, size), 0) >= lax.broadcasted_iota(
        jnp.int32, (size, size), 1
    )


def ring_columns(w_ref, out_ref, hops, sem):
    width = w_ref.shape[1] // lax.axis_size("head")
    copies = []
    for j in range(out_ref.shape[1] // width):
        here = pl.ds(j * width, width)
        copies.append(pltpu.make_async_copy(w_ref.at[:, columns_after(hops + j, width)], out_ref.at[:, here], sem.at[j]))
        copies[-1].start()
    return copies


def contrib_kernel(groups, k_ref, v_ref, ld_ref, w_ref, state_ref, row_ref, col_ref, first_ref, rest_ref, sem):
    count = first_ref.shape[1] * lax.axis_size("head") // w_ref.shape[1]
    copies = ring_columns(w_ref, first_ref, 1, sem) + ring_columns(w_ref, rest_ref, 1 + count, sem.at[pl.ds(count, sem.shape[0] - count)])
    size = k_ref.shape[0]
    lower = lower_mask(size).astype(F32)
    ld = ld_ref[...]
    row = lax.dot_general(
        ld, lower, (((1,), (1,)), ((), ())), precision=lax.Precision.HIGHEST, preferred_element_type=F32
    )
    col = lax.dot_general(
        lower, ld, (((1,), (1,)), ((), ())), precision=lax.Precision.HIGHEST, preferred_element_type=F32
    )
    row_ref[...] = row
    col_ref[...] = col
    tail = jnp.exp(col[size - 1 :, :] - col)
    for h in range(groups):
        weighted = (head(k_ref, h).astype(F32) * tail[:, h : h + 1]).astype(BF16)
        state_ref[h * DH : (h + 1) * DH, :] = contract(weighted, head(v_ref, h), 0, 0).astype(BF16)
    store_decay(state_ref, row, groups)
    for copy in copies:
        copy.wait()


def spread_weights(row_ref, col_ref, lower, h):
    spread = col_ref[:, h : h + 1] - row_ref[h : h + 1, :]
    return jnp.exp(jnp.where(lower, spread, -jnp.inf))


def again_kernel(ref, again_ref):
    again_ref[...] = ref[...]


def intra_kernel(groups, q_ref, k_ref, v_ref, row_ref, col_ref, intra_ref):
    lower = lower_mask(q_ref.shape[0])
    for h in range(groups):
        weights = spread_weights(row_ref, col_ref, lower, h)
        probs = (contract(head(q_ref, h), head(k_ref, h), 1, 1) * SCALE * weights).astype(BF16)
        intra_ref[:, h * DH : (h + 1) * DH] = contract(probs, head(v_ref, h), 1, 0)


def attended_kernel(groups, count, *refs):
    states = refs[:count]
    q_ref, intra_ref, col_ref, pick_own_ref, pick_other_ref, rest_ref = refs[count : count + 6]
    own_ref, other_ref, low_ref, again_ref, attended_ref = refs[count + 6 :]
    again_ref[...] = rest_ref[...]
    state = entering(states, groups, True)
    factor = jnp.exp(col_ref[...]) * SCALE
    for h in range(groups):
        low = state(h).astype(BF16)
        low_ref[h] = low
        inter = contract(head(q_ref, h), low, 1, 0)
        attended_ref[:, h * DH : (h + 1) * DH] = (
            head(intra_ref, h) + inter * factor[:, h : h + 1]
        ).astype(BF16)
    own_ref[...] = contract(attended_ref[...], pick_own_ref[...], 1, 0).astype(BF16)
    other_ref[...] = contract(attended_ref[...], pick_other_ref[...], 1, 0).astype(BF16)


def back_contrib_kernel(
    groups, own_ref, other_ref, pick_own_ref, pick_other_ref, q_ref, row_ref, col_ref, grad_ref, state_ref
):
    grad_ref[...] = (
        contract(own_ref[...], pick_own_ref[...], 1, 1) + contract(other_ref[...], pick_other_ref[...], 1, 1)
    ).astype(BF16)
    factor = jnp.exp(col_ref[...]) * SCALE
    for h in range(groups):
        weighted = (head(q_ref, h).astype(F32) * factor[:, h : h + 1]).astype(BF16)
        state_ref[h * DH : (h + 1) * DH, :] = contract(weighted, head(grad_ref, h), 0, 0).astype(BF16)
    store_decay(state_ref, row_ref[...], groups)


def back_intra_kernel(
    groups, grad_ref, q_ref, k_ref, v_ref, row_ref, col_ref, low_ref, qgrad_ref, kpart_ref, vpart_ref
):
    lower = lower_mask(q_ref.shape[0])
    factor = jnp.exp(col_ref[...]) * SCALE
    for h in range(groups):
        here = slice(h * DH, (h + 1) * DH)
        grad = head(grad_ref, h)
        weights = spread_weights(row_ref, col_ref, lower, h)
        dprobs = (contract(grad, head(v_ref, h), 1, 1) * SCALE * weights).astype(BF16)
        qgrad_ref[:, here] = (
            contract(dprobs, head(k_ref, h), 1, 0) + contract(grad, low_ref[h], 1, 1) * factor[:, h : h + 1]
        ).astype(BF16)
        kpart_ref[:, here] = contract(dprobs, head(q_ref, h), 0, 0)
        probs = (contract(head(q_ref, h), head(k_ref, h), 1, 1) * SCALE * weights).astype(BF16)
        vpart_ref[:, here] = contract(probs, grad, 0, 0)


def back_inter_kernel(groups, count, *refs):
    states = refs[:count]
    k_ref, v_ref, col_ref, kpart_ref, vpart_ref, kgrad_ref, vgrad_ref = refs[count:]
    state = entering(states, groups, False)
    col = col_ref[...]
    tail = jnp.exp(col[col.shape[0] - 1 :, :] - col)
    for h in range(groups):
        here = slice(h * DH, (h + 1) * DH)
        low = state(h).astype(BF16)
        kgrad_ref[:, here] = (
            head(kpart_ref, h) + tail[:, h : h + 1] * contract(head(v_ref, h), low, 1, 1)
        ).astype(BF16)
        vgrad_ref[:, here] = (
            head(vpart_ref, h) + tail[:, h : h + 1] * contract(head(k_ref, h), low, 1, 0)
        ).astype(BF16)


def hops_of(state, forward):
    devices = lax.axis_size("ctx")
    out = []
    for hop in range(1, devices):
        if forward:
            pairs = [(i, i + hop) for i in range(devices - hop)]
        else:
            pairs = [(i + hop, i) for i in range(devices - hop)]
        out.append(lax.ppermute(state, "ctx", pairs))
    return out


def swapped(array):
    return lax.ppermute(array, "dp", [(0, 1), (1, 0)])


def flipped(array, bit):
    return lax.ppermute(array, "ctx", [(i, i ^ bit) for i in range(4)])


def rows_kernel(one, two, on_one, on_two):
    half = on_one.shape[0]
    on_one[...] = one[:half]
    on_two[...] = two[half:]


def lay_out(pieces, out_ref, columns=slice(None)):
    top = 0
    for piece in pieces:
        out_ref[top : top + piece.shape[0], :] = piece[:, columns]
        top += piece.shape[0]


def columns_after(hops, width):
    devices = lax.axis_size("head")
    return pl.ds(pl.multiple_of(lax.rem(lax.axis_index("head") + hops, devices) * width, width), width)


def mix_kernel(count, place, splits, a_own, a_other, *refs):
    pieces, owns, others, w_ref = refs[:count], refs[count : -1 - splits], refs[-1 - splits : -1], refs[-1]
    width = w_ref.shape[1]
    away = []
    for j, own in enumerate(owns):
        lay_out(pieces, w_ref, slice((place + j) * width, (place + j + 1) * width))
        own[...] = contract(a_own[...], w_ref[...], 1, 0)
        away.append(contract(a_other[...], w_ref[...], 1, 0).astype(BF16))
    away = away[0] if len(away) == 1 else jnp.concatenate(away, axis=1)
    for i, other in enumerate(others):
        other[...] = away[:, i * other.shape[1] : (i + 1) * other.shape[1]]


def grad_kernel(count, earlier, g_own, g_other, *refs):
    first, rest, (own, other, w_ref) = refs[:count], refs[count : 2 * count], refs[2 * count + earlier :]
    heads = lax.axis_size("head")
    left, width = first[0].shape[1], w_ref.shape[1] // heads
    lay_out(first, w_ref.at[:, 0:left])
    lay_out(rest, w_ref.at[:, left:])
    before = refs[2 * count : 2 * count + earlier] or (None, None)
    for g_ref, old, out in ((g_own, before[0], own), (g_other, before[1], other)):
        total = None
        for j in range(heads):
            term = contract(
                g_ref[:, columns_after(1 + j, width)], w_ref[:, j * width : (j + 1) * width], 1, 1
            )
            total = term if total is None else total + term
        if old is not None:
            out[:, : old.shape[1]] = old[...]
        out[:, out.shape[1] - total.shape[1] :] = total.astype(BF16)


def weight_kernel(blocks, a_own, a_other, g_own, g_other, *outs):
    rows = a_own.shape[1] // 4
    for (k, left, right), out in zip(blocks, outs):
        here = slice(k * rows, (k + 1) * rows)
        out[...] = (
            contract(a_own[:, here], g_own[:, left:right], 0, 0)
            + contract(a_other[:, here], g_other[:, left:right], 0, 0)
        ).astype(out.dtype)


def onward_kernel(mid_left, mid_right, far_left, far_right, left_ref, right_ref):
    left_ref[...] = (mid_left[...] + far_left[...].astype(F32)).astype(BF16)
    right_ref[...] = (mid_right[...] + far_right[...].astype(F32)).astype(BF16)


def total_kernel(own_ref, left_ref, right_ref, out_ref):
    half = own_ref.shape[1] // 2
    left, right = slice(0, half), slice(half, 2 * half)
    out_ref[:, left] = own_ref[:, left] + left_ref[...].astype(F32)
    out_ref[:, right] = own_ref[:, right] + right_ref[...].astype(F32)


def back_pair_kernel(groups, own_ref, near_ref, left_ref, right_ref, out_ref, left_again, right_again):
    left_again[...] = left_ref[...]
    right_again[...] = right_ref[...]
    pair_kernel(groups, False, own_ref, near_ref, out_ref)


def ring_kernel(j, count, own_ref, *refs):
    width = own_ref.shape[1]
    other = [ref[...] for ref in refs[:count]]
    other = other[0] if count == 1 else jnp.concatenate(other, axis=1)
    total = own_ref[...] + other[:, j * width : (j + 1) * width].astype(F32)
    if len(refs) == count + 2:
        total = total + refs[count][...].astype(F32)
    refs[-1][...] = total.astype(BF16)


def passed(array):
    devices = lax.axis_size("head")
    return lax.ppermute(array, "head", [(i, (i - 1) % devices) for i in range(devices)])


def picks(groups, rows_each):
    devices, mine, core = lax.axis_size("ctx"), lax.axis_index("ctx"), lax.axis_index("dp")
    width = devices * rows_each * groups
    feature = lax.broadcasted_iota(jnp.int32, (groups * DH, width), 0)
    place = lax.broadcasted_iota(jnp.int32, (groups * DH, width), 1)
    block = place // (rows_each * groups)
    if devices == 4:
        block = block ^ mine
    row = (place // groups) % rows_each
    group = place % groups

    def pick(p):
        return (feature == group * DH + (block * 2 + p) * rows_each + row).astype(BF16)

    return pick(core), pick(1 - core)


def shards(queries, keys, values, log_decay, w_out, grad_out):
    groups = log_decay.shape[1]
    size = queries.shape[1]
    devices, heads = lax.axis_size("ctx"), lax.axis_size("head")
    four = devices == 4
    q, k, v, ld, g = queries[0], keys[0], values[0], log_decay[0], grad_out[0]
    rows_each, _, width = w_out.shape
    rows, part, middle = rows_each * groups, width // heads, width // 2
    w = w_out.reshape(rows, width)
    features = groups * DH
    state_shape = struct((features + EXTRA, DH), BF16)
    flat = lambda dtype: struct((size, features), dtype)
    half = struct((size, features // 2), BF16)
    last = []

    def step(kernel, out_shape, *args, after=(), **kwargs):
        out = call(kernel, out_shape, *args, after=[*last, *after], **kwargs)
        last[:] = [min(jax.tree.leaves(out), key=lambda x: x.size)]
        return out

    near_heads = heads // 2
    first_shape, rest_shape = (struct((rows, count * part), BF16) for count in (near_heads, heads - near_heads))
    state, row, col, w_first, w_rest = step(
        functools.partial(contrib_kernel, groups),
        (state_shape, struct((groups, size), F32), struct((size, groups), F32), first_shape, rest_shape),
        k,
        v,
        ld,
        w,
        staged=(0, 1, 2),
        free_in=(3,),
        scratch=[pltpu.SemaphoreType.DMA((heads,))],
        room=60,
    )
    g_other = swapped(g)
    if four:
        near = flipped(state, 1)
        first_two = flipped(w_first, 2)
        w_again = step(again_kernel, first_shape, w_first)
        first_one = flipped(w_again, 1)
    else:
        before = hops_of(state, True)
    pick_own, pick_other = picks(groups, rows_each)
    intra = step(
        functools.partial(intra_kernel, groups),
        flat(F32),
        q,
        k,
        v,
        row,
        col,
        staged=(0, 1, 2),
        after=[g_other],
    )
    if four:
        pair = step(functools.partial(pair_kernel, groups, True), struct((features, DH), BF16), state, near)
        before = [near, lax.ppermute(pair, "ctx", [(0, 2), (1, 3)])]
        lower = lambda array: struct((rows // 2, array.shape[1]), BF16)
        on_one, on_two = step(rows_kernel, [lower(w_first)] * 2, first_one, first_two)
        first = [w_first, first_one, first_two, flipped(on_one, 2), flipped(on_two, 1)]
    else:
        first = [lax.all_gather(w_first, "ctx", axis=0, tiled=True)]
        rest = [lax.all_gather(w_rest, "ctx", axis=0, tiled=True)]
    a_own, a_away, low, w_again = step(
        functools.partial(attended_kernel, groups, len(before)),
        (half, half, struct((groups, DH, DH), BF16), rest_shape),
        *before,
        q,
        intra,
        col,
        pick_own,
        pick_other,
        w_rest,
        scratch=[pltpu.VMEM((size, features), BF16)],
    )
    a_other = swapped(a_away)
    held = pltpu.VMEM((features // 2, part), BF16)

    def mix(pieces, place, count, splits=1, work=0):
        out = step(
            functools.partial(mix_kernel, len(pieces), place, splits),
            [struct((size, part), F32)] * count + [struct((size, count * part // splits), BF16)] * splits,
            a_own,
            a_other,
            *pieces,
            scratch=[held],
            work=work,
        )
        away = [swapped(other) for other in out[count:]]
        return [(own, away, j) for j, own in enumerate(out[:count])]

    def ring(terms, *arrived, work=0):
        own, away, j = terms
        return step(
            functools.partial(ring_kernel, j, len(away)), struct((size, part), BF16), own, *away, *arrived, work=work
        )

    def weights(blocks, shapes):
        return step(functools.partial(weight_kernel, blocks), shapes, a_own, a_other, g, g_other)

    def grad_of(some, *earlier):
        here = sum(piece.shape[0] for piece, _ in some)
        wide = here + sum(array.shape[1] for array in earlier[:1])
        return step(
            functools.partial(grad_kernel, len(some), len(earlier)),
            [struct((size, wide), BF16)] * 2,
            g,
            g_other,
            *[piece for piece, _ in some],
            *[piece for _, piece in some],
            *earlier,
            scratch=[pltpu.VMEM((here, width), BF16)],
        )

    if four:
        small = lambda dtype: struct((rows, middle), dtype)
        blocks = [
            (3, 0, middle), (3, middle, width), (2, 0, middle), (1, middle, width), (1, 0, middle), (2, middle, width), (0, 0, width),
        ]
        *far, mid_left, mid_right, near_left, near_right, own_sum = weights(
            blocks, [small(BF16)] * 2 + [small(F32)] * 2 + [small(BF16)] * 2 + [struct((rows, width), F32)]
        )
    terms = mix(first, 0, near_heads, 3 if four else 1, 0)
    arrived = passed(ring(terms[0]))
    if four:
        rest_one, rest_two = flipped(w_again, 1), flipped(w_again, 2)
        on_one, on_two = step(rows_kernel, [lower(w_rest)] * 2, rest_one, rest_two)
        rest = [w_rest, rest_one, rest_two, flipped(on_one, 2), flipped(on_two, 1)]
        far_left, far_right = flipped(far[0], 1), flipped(far[1], 2)
        both = list(zip(first, rest))
        grad_own, grad_away = grad_of(both[3:], *grad_of(both[:3]))
    else:
        grad_own, grad_away = grad_of(list(zip(first, rest)))
    grad_other = swapped(grad_away)
    for j in range(1, near_heads):
        arrived = passed(ring(terms[j], arrived, work=C17))
    grad, back = step(
        functools.partial(back_contrib_kernel, groups),
        (flat(BF16), state_shape),
        grad_own,
        grad_other,
        pick_own,
        pick_other,
        q,
        row,
        col,
    )
    if four:
        near = flipped(back, 1)
    else:
        after = hops_of(back, False)
    if four:
        to_left, to_right = step(onward_kernel, [small(BF16)] * 2, mid_left, mid_right, far_left, far_right)
        on_left, on_right = flipped(to_left, 2), flipped(to_right, 1)
    terms = mix(rest, 0, 1)
    if four:
        pair, near_left, near_right = step(
            functools.partial(back_pair_kernel, groups),
            [struct((features, DH), BF16), small(BF16), small(BF16)],
            back,
            near,
            near_left,
            near_right,
            work=C20,
        )
        after = [near, lax.ppermute(pair, "ctx", [(2, 0), (3, 1)])]
        near_left, near_right = flipped(near_left, 1), flipped(near_right, 2)
    query_grad, key_part, value_part = step(
        functools.partial(back_intra_kernel, groups),
        (flat(BF16), flat(F32), flat(F32)),
        grad,
        q,
        k,
        v,
        row,
        col,
        low,
        staged=(1, 2, 3),
    )
    for j in range(1, heads - near_heads):
        arrived = passed(ring(terms[0], arrived))
        terms = mix(rest, j, 1)
    if four:
        own_sum = step(total_kernel, struct((rows, width), F32), own_sum, on_left, on_right)
    key_grad, value_grad = step(
        functools.partial(back_inter_kernel, groups, len(after)),
        (flat(BF16), flat(BF16)),
        *after,
        k,
        v,
        col,
        key_part,
        value_part,
        work=C24,
    )
    if four:
        w_grad = step(total_kernel, struct((rows, width), F32), own_sum, near_left, near_right)
    else:
        w_grad = contract(a_own, g, 0, 0) + contract(a_other, g_other, 0, 0)
        w_grad = lax.psum_scatter(w_grad.astype(BF16), "ctx", scatter_dimension=0, tiled=True).astype(F32)
    mixed = ring(terms[0], arrived)
    return (
        mixed[None],
        query_grad[None],
        key_grad[None],
        value_grad[None],
        w_grad.reshape(rows_each, groups, width),
    )


def solution(mesh):
    return jax.shard_map(
        shards,
        mesh=mesh,
        in_specs=(
            P("dp", "ctx", "head"),
            P("dp", "ctx", "head"),
            P("dp", "ctx", "head"),
            P("dp", "head", "ctx"),
            P(("ctx", "dp"), "head", None),
            P("dp", "ctx", None),
        ),
        out_specs=(
            P("dp", "ctx", "head"),
            P("dp", "ctx", "head"),
            P("dp", "ctx", "head"),
            P("dp", "ctx", "head"),
            P(("ctx", "dp"), "head", None),
        ),
        check_vma=False,
    )
```

```python
import functools

import jax
import jax.numpy as jnp
from jax import lax
from jax.experimental import pallas as pl
from jax.experimental.pallas import tpu as pltpu
from jax.sharding import PartitionSpec as P

DH = 128
SCALE = 1.0 / DH
F32 = jnp.float32
BF16 = jnp.bfloat16
EXTRA = 16
C_JOIN, C26, C17, C20, C24 = 1070000000, 642000000, 1284000000, 1070000000, 2140000000


def contract(a, b, dim_a, dim_b):
    return lax.dot_general(a, b, (((dim_a,), (dim_b,)), ((), ())), preferred_element_type=F32)


def head(ref, h):
    return ref[:, h * DH : (h + 1) * DH]


def call(kernel, out_shape, *args, staged=(), free_in=(), scratch=(), after=(), room=24, work=0):
    outs = list(out_shape) if isinstance(out_shape, (list, tuple)) else [out_shape]
    n, waits, count, made = len(args), len(after), len(staged), len(outs)

    def body(*refs):
        ins, rest = list(refs[:n]), refs[n + waits :]
        results, rest = rest[: made + 1], rest[made + 1 :]
        rest, buffers, sem = rest[: len(rest) - count - 1], rest[len(rest) - count - 1 : -1], rest[-1]
        copies = [pltpu.make_async_copy(ins[i], buffers[j], sem.at[j]) for j, i in enumerate(staged)]
        for copy in copies:
            copy.start()
        results[-1][...] = jnp.zeros_like(results[-1])
        for copy in copies:
            copy.wait()
        for j, i in enumerate(staged):
            ins[i] = buffers[j]
        kernel(*ins, *results[:-1], *rest)

    anywhere, local, far = (pl.BlockSpec(memory_space=m) for m in (pl.ANY, pltpu.VMEM, pltpu.HBM))
    results = pl.pallas_call(
        body,
        name=getattr(kernel, "func", kernel).__name__,
        out_shape=[*outs, struct((8, 128), F32)],
        in_specs=[far if i in staged or i in free_in else local for i in range(n)] + [anywhere] * waits,
        out_specs=[local] * (made + 1),
        scratch_shapes=[
            *scratch,
            *[pltpu.VMEM(args[i].shape, args[i].dtype) for i in staged],
            pltpu.SemaphoreType.DMA((max(count, 1),)),
        ],
        compiler_params=pltpu.CompilerParams(vmem_limit_bytes=room * 1024 * 1024),
        cost_estimate=pl.CostEstimate(flops=work, bytes_accessed=0, transcendentals=0),
    )(*args, *after)
    return (results[:-1] if isinstance(out_shape, (list, tuple)) else results[0]), results[-1]


def struct(shape, dtype):
    return jax.ShapeDtypeStruct(shape, dtype)


def store_decay(out_ref, row, groups):
    decay = jnp.broadcast_to(jnp.exp(row[:, -1:]), (groups, DH))
    high = decay.astype(BF16).astype(F32)
    both = jnp.concatenate([high, decay - high], axis=0)
    out_ref[groups * DH : groups * DH + EXTRA, :] = both.astype(BF16)


def load_decay(ref, groups):
    both = ref[groups * DH : groups * DH + EXTRA, :].astype(F32)
    return both[:groups] + both[groups:]


def entering(refs, groups, forward):
    if lax.axis_size("ctx") == 4:
        near, far = refs
        bit = side(forward)
        decay = load_decay(near, groups) * bit + (1.0 - bit)
        return lambda h: rows_of(near, h) * bit + decay[h : h + 1, :] * rows_of(far, h)
    decays = [load_decay(ref, groups) for ref in refs[:-1]]

    def state(h):
        total = rows_of(refs[-1], h)
        for ref, decay in zip(refs[-2::-1], decays[::-1]):
            total = rows_of(ref, h) + decay[h : h + 1, :] * total
        return total

    return state


def rows_of(ref, h):
    return ref[h * DH : (h + 1) * DH, :].astype(F32)


def side(forward):
    bit = lax.rem(lax.axis_index("ctx"), 2).astype(F32)
    return bit if forward else 1.0 - bit


def pair_kernel(groups, forward, own_ref, near_ref, *refs):
    out_ref = refs[-1]
    if len(refs) == 3:
        refs[1][...] = refs[0][...]
    bit = side(forward)
    own_decay, near_decay = load_decay(own_ref, groups), load_decay(near_ref, groups)
    for h in range(groups):
        here = slice(h, h + 1)
        own, near = rows_of(own_ref, h), rows_of(near_ref, h)
        own_share = bit + (1.0 - bit) * near_decay[here]
        near_share = bit * own_decay[here] + (1.0 - bit)
        out_ref[h * DH : (h + 1) * DH, :] = (own_share * own + near_share * near).astype(BF16)


def lower_mask(size):
    return lax.broadcasted_iota(jnp.int32, (size, size), 0) >= lax.broadcasted_iota(
        jnp.int32, (size, size), 1
    )


def ring_columns(w_ref, out_ref, hops, sem):
    width = w_ref.shape[1] // lax.axis_size("head")
    copies = []
    for j in range(out_ref.shape[1] // width):
        here = pl.ds(j * width, width)
        copies.append(pltpu.make_async_copy(w_ref.at[:, columns_after(hops + j, width)], out_ref.at[:, here], sem.at[j]))
        copies[-1].start()
    return copies


def columns_kernel(w_ref, first_ref, rest_ref, sem):
    count = first_ref.shape[1] * lax.axis_size("head") // w_ref.shape[1]
    copies = ring_columns(w_ref, first_ref, 1, sem)
    copies += ring_columns(w_ref, rest_ref, 1 + count, sem.at[pl.ds(count, sem.shape[0] - count)])
    for copy in copies:
        copy.wait()


def sums(ld_ref, mask, rows):
    lower = mask.astype(F32)
    a, b = (lower, ld_ref[...]) if rows else (ld_ref[...], lower)
    return lax.dot_general(
        a, b, (((1,), (1,)), ((), ())), precision=lax.Precision.HIGHEST, preferred_element_type=F32
    )


def contrib_kernel(groups, k_ref, v_ref, ld_ref, state_ref):
    size = k_ref.shape[0]
    mask = lower_mask(size)
    col = sums(ld_ref, mask, True)
    tail = jnp.exp(col[size - 1 :, :] - col)
    for h in range(groups):
        weighted = (head(k_ref, h).astype(F32) * tail[:, h : h + 1]).astype(BF16)
        state_ref[h * DH : (h + 1) * DH, :] = contract(weighted, head(v_ref, h), 0, 0).astype(BF16)
    store_decay(state_ref, sums(ld_ref, mask, False), groups)


def intra_kernel(groups, q_ref, k_ref, v_ref, ld_ref, row_ref, col_ref, intra_ref):
    mask = lower_mask(q_ref.shape[0])
    row_ref[...] = sums(ld_ref, mask, False)
    col_ref[...] = sums(ld_ref, mask, True)
    for h in range(groups):
        probs = probs_of(q_ref, k_ref, spread_weights(row_ref, col_ref, mask, h), h)
        intra_ref[:, h * DH : (h + 1) * DH] = contract(probs, head(v_ref, h), 1, 0)


def probs_of(q_ref, k_ref, weights, h):
    return (contract(head(q_ref, h), head(k_ref, h), 1, 1) * SCALE * weights).astype(BF16)


def spread_weights(row_ref, col_ref, lower, h):
    spread = col_ref[:, h : h + 1] - row_ref[h : h + 1, :]
    return jnp.exp(jnp.where(lower, spread, -jnp.inf))


def attended_kernel(groups, count, *refs):
    states = refs[:count]
    q_ref, intra_ref, col_ref, pick_own_ref, pick_other_ref, g_ref = refs[count : count + 6]
    own_ref, other_ref, low_ref, held_ref, attended_ref, sem = refs[count + 6 :]
    copy = pltpu.make_async_copy(g_ref, held_ref, sem.at[0])
    copy.start()
    state = entering(states, groups, True)
    factor = jnp.exp(col_ref[...]) * SCALE
    for h in range(groups):
        low = state(h).astype(BF16)
        low_ref[h] = low
        inter = contract(head(q_ref, h), low, 1, 0)
        attended_ref[:, h * DH : (h + 1) * DH] = (
            head(intra_ref, h) + inter * factor[:, h : h + 1]
        ).astype(BF16)
    own_ref[...] = contract(attended_ref[...], pick_own_ref[...], 1, 0).astype(BF16)
    other_ref[...] = contract(attended_ref[...], pick_other_ref[...], 1, 0).astype(BF16)
    copy.wait()


def back_contrib_kernel(
    groups, own_ref, other_ref, pick_own_ref, pick_other_ref, q_ref, row_ref, col_ref, grad_ref, state_ref
):
    grad_ref[...] = (
        contract(own_ref[...], pick_own_ref[...], 1, 1) + contract(other_ref[...], pick_other_ref[...], 1, 1)
    ).astype(BF16)
    factor = jnp.exp(col_ref[...]) * SCALE
    for h in range(groups):
        weighted = (head(q_ref, h).astype(F32) * factor[:, h : h + 1]).astype(BF16)
        state_ref[h * DH : (h + 1) * DH, :] = contract(weighted, head(grad_ref, h), 0, 0).astype(BF16)
    store_decay(state_ref, row_ref[...], groups)


def back_intra_kernel(
    groups, grad_ref, q_ref, k_ref, v_ref, row_ref, col_ref, low_ref, qgrad_ref, kpart_ref, vpart_ref
):
    lower = lower_mask(q_ref.shape[0])
    factor = jnp.exp(col_ref[...]) * SCALE
    for h in range(groups):
        here = slice(h * DH, (h + 1) * DH)
        grad = head(grad_ref, h)
        weights = spread_weights(row_ref, col_ref, lower, h)
        dprobs = (contract(grad, head(v_ref, h), 1, 1) * SCALE * weights).astype(BF16)
        qgrad_ref[:, here] = (
            contract(dprobs, head(k_ref, h), 1, 0) + contract(grad, low_ref[h], 1, 1) * factor[:, h : h + 1]
        ).astype(BF16)
        kpart_ref[:, here] = contract(dprobs, head(q_ref, h), 0, 0)
        probs = probs_of(q_ref, k_ref, weights, h)
        vpart_ref[:, here] = contract(probs, grad, 0, 0)


def back_inter_kernel(groups, count, *refs):
    states = refs[:count]
    k_ref, v_ref, col_ref, kpart_ref, vpart_ref, kgrad_ref, vgrad_ref = refs[count:]
    state = entering(states, groups, False)
    col = col_ref[...]
    tail = jnp.exp(col[col.shape[0] - 1 :, :] - col)
    for h in range(groups):
        here = slice(h * DH, (h + 1) * DH)
        low = state(h).astype(BF16)
        kgrad_ref[:, here] = (
            head(kpart_ref, h) + tail[:, h : h + 1] * contract(head(v_ref, h), low, 1, 1)
        ).astype(BF16)
        vgrad_ref[:, here] = (
            head(vpart_ref, h) + tail[:, h : h + 1] * contract(head(k_ref, h), low, 1, 0)
        ).astype(BF16)


def hops_of(state, forward):
    devices = lax.axis_size("ctx")
    out = []
    for hop in range(1, devices):
        if forward:
            pairs = [(i, i + hop) for i in range(devices - hop)]
        else:
            pairs = [(i + hop, i) for i in range(devices - hop)]
        out.append(lax.ppermute(state, "ctx", pairs))
    return out


def swapped(array):
    return lax.ppermute(array, "dp", [(0, 1), (1, 0)])


def flipped(array, bit):
    return lax.ppermute(array, "ctx", [(i, i ^ bit) for i in range(4)])


def pass_kernel(one, two, whole, on_one, on_two, again):
    again[...] = whole[...]
    rows_kernel(one, two, on_one, on_two)


def rows_kernel(one, two, on_one, on_two):
    half = on_one.shape[0]
    on_one[...] = one[:half]
    on_two[...] = two[half:]


def join_kernel(*refs):
    lay_out(refs[:-1], refs[-1])


def lay_out(pieces, out_ref, columns=slice(None)):
    top = 0
    for piece in pieces:
        out_ref[top : top + piece.shape[0], :] = piece[:, columns]
        top += piece.shape[0]


def along(place):
    return place ^ (place >> 1) if lax.axis_size("head") == 4 else place


def columns_after(hops, width):
    devices = lax.axis_size("head")
    device = along(lax.rem(along(lax.axis_index("head")) + hops, devices))
    return pl.ds(pl.multiple_of(device * width, width), width)


def mix_kernel(count, place, splits, a_own, a_other, *refs):
    pieces, owns, others, w_ref = refs[:count], refs[count : -1 - splits], refs[-1 - splits : -1], refs[-1]
    width = w_ref.shape[1]
    away = []
    for j, own in enumerate(owns):
        lay_out(pieces, w_ref, slice((place + j) * width, (place + j + 1) * width))
        own[...] = contract(a_own[...], w_ref[...], 1, 0)
        away.append(contract(a_other[...], w_ref[...], 1, 0).astype(BF16))
    away = away[0] if len(away) == 1 else jnp.concatenate(away, axis=1)
    for i, other in enumerate(others):
        other[...] = away[:, i * other.shape[1] : (i + 1) * other.shape[1]]


def grad_kernel(top, count, earlier, g_own, g_other, first_ref, *refs):
    pieces, before, (own, other, w_ref) = refs[:count], refs[count : count + earlier], refs[count + earlier :]
    heads = lax.axis_size("head")
    rows, left, width = w_ref.shape[0], first_ref.shape[1], w_ref.shape[1] // heads
    w_ref[:, :left] = first_ref[top : top + rows]
    lay_out(pieces, w_ref.at[:, left:])
    for g_ref, old, out in ((g_own, before[:1], own), (g_other, before[1:], other)):
        total = None
        for j in range(heads):
            term = contract(
                g_ref[:, columns_after(1 + j, width)], w_ref[:, j * width : (j + 1) * width], 1, 1
            )
            total = term if total is None else total + term
        start = out.shape[1] - rows
        if old:
            out[:, :start] = old[0][...]
        out[:, start:] = total.astype(BF16)


def weight_kernel(blocks, a_own, a_other, g_own, g_other, *outs):
    rows = a_own.shape[1] // 4
    for (k, left, right), out in zip(blocks, outs):
        here = slice(k * rows, (k + 1) * rows)
        out[...] = (
            contract(a_own[:, here], g_own[:, left:right], 0, 0)
            + contract(a_other[:, here], g_other[:, left:right], 0, 0)
        ).astype(out.dtype)


def onward_kernel(mid_left, mid_right, far_left, far_right, left_ref, right_ref):
    left_ref[...] = (mid_left[...] + far_left[...].astype(F32)).astype(BF16)
    right_ref[...] = (mid_right[...] + far_right[...].astype(F32)).astype(BF16)


def total_kernel(parts, own_ref, *refs):
    half = own_ref.shape[1] // 2
    out_ref = refs[-1]
    sides = [own_ref[:, :half], own_ref[:, half:]]
    for left, ref in zip(parts, refs[:-1]):
        sides[left] = sides[left] + ref[...].astype(F32)
    out_ref[:, :half], out_ref[:, half:] = sides


def back_pair_kernel(groups, own_ref, near_ref, left_ref, right_ref, out_ref, left_again, right_again):
    left_again[...] = left_ref[...]
    right_again[...] = right_ref[...]
    pair_kernel(groups, False, own_ref, near_ref, out_ref)


def ring_kernel(j, count, own_ref, *refs):
    width = own_ref.shape[1]
    other = [ref[...] for ref in refs[:count]]
    other = other[0] if count == 1 else jnp.concatenate(other, axis=1)
    total = own_ref[...] + other[:, j * width : (j + 1) * width].astype(F32)
    if len(refs) == count + 2:
        total = total + refs[count][...].astype(F32)
    refs[-1][...] = total.astype(BF16)


def passed(array):
    devices = lax.axis_size("head")
    pairs = [(along(i), along((i - 1) % devices)) for i in range(devices)]
    return lax.ppermute(array, "head", pairs)


def picks_kernel(groups, rows_each, own_ref, other_ref):
    devices, mine, core = lax.axis_size("ctx"), lax.axis_index("ctx"), lax.axis_index("dp")
    width = own_ref.shape[1]
    shape = (DH, width)
    feature, place = lax.broadcasted_iota(jnp.int32, shape, 0), lax.broadcasted_iota(jnp.int32, shape, 1)
    block = place // (rows_each * groups)
    if devices == 4:
        block = block ^ mine
    row = (place // groups) % rows_each
    for p, ref in ((core, own_ref), (1 - core, other_ref)):
        match = feature == (block * 2 + p) * rows_each + row
        for h in range(groups):
            ref[h * DH : (h + 1) * DH, :] = (match & (place % groups == h)).astype(F32).astype(BF16)


def shards(queries, keys, values, log_decay, w_out, grad_out):
    groups = log_decay.shape[1]
    size = queries.shape[1]
    devices, heads = lax.axis_size("ctx"), lax.axis_size("head")
    four = devices == 4
    q, k, v, ld, g = queries[0], keys[0], values[0], log_decay[0], grad_out[0]
    rows_each, _, width = w_out.shape
    rows, part, middle = rows_each * groups, width // heads, width // 2
    w = w_out.reshape(rows, width)
    features = groups * DH
    state_shape = struct((features + EXTRA, DH), BF16)
    flat = lambda dtype: struct((size, features), dtype)
    half = struct((size, features // 2), BF16)
    last = []

    def step(kernel, out_shape, *args, after=(), **kwargs):
        out, done = call(kernel, out_shape, *args, after=[*last, *after], **kwargs)
        last[:] = [done]
        return out

    near_heads = heads // 2
    first_shape, rest_shape = (struct((rows, count * part), BF16) for count in (near_heads, heads - near_heads))
    state = step(
        functools.partial(contrib_kernel, groups), state_shape, k, v, ld, staged=(0, 1, 2), room=60
    )
    w_first, w_rest = step(
        columns_kernel,
        [first_shape, rest_shape],
        w,
        free_in=(0,),
        scratch=[pltpu.SemaphoreType.DMA((heads,))],
        room=60,
    )
    g_other = swapped(g)
    if four:
        near = flipped(state, 1)
        first_two, first_one = flipped(w_first, 2), flipped(w_first, 1)
        pair = step(functools.partial(pair_kernel, groups, True), struct((features, DH), BF16), state, near)
        before = [near, lax.ppermute(pair, "ctx", [(0, 2), (1, 3)])]
        lower = lambda array: struct((rows // 2, array.shape[1]), BF16)
    pick_own, pick_other = step(
        functools.partial(picks_kernel, groups, rows_each),
        [struct((features, features // 2), BF16)] * 2,
        after=[g_other],
    )
    row, col, intra = step(
        functools.partial(intra_kernel, groups),
        (struct((groups, size), F32), struct((size, groups), F32), flat(F32)),
        q,
        k,
        v,
        ld,
    )
    if four:
        on_one, on_two, w_again = step(
            pass_kernel, [lower(w_first)] * 2 + [rest_shape], first_one, first_two, w_rest
        )
        first = [w_first, first_one, first_two, flipped(on_one, 2), flipped(on_two, 1)]
    else:
        before = hops_of(state, True)
        first = lax.all_gather(w_first, "ctx", axis=0, tiled=True)
        rest = [lax.all_gather(w_rest, "ctx", axis=0, tiled=True)]
    a_own, a_away, low, g_own = step(
        functools.partial(attended_kernel, groups, len(before)),
        (half, half, struct((groups, DH, DH), BF16), struct(g.shape, BF16)),
        *before,
        q,
        intra,
        col,
        pick_own,
        pick_other,
        g,
        free_in=(len(before) + 5,),
        scratch=[pltpu.VMEM((size, features), BF16), pltpu.SemaphoreType.DMA((1,))],
    )
    a_other = swapped(a_away)
    if four:
        first = step(join_kernel, struct((devices * rows, first_shape.shape[1]), BF16), *first, work=C_JOIN)
    held = pltpu.VMEM((features // 2, part), BF16)

    def mix(pieces, place, count, splits=1, work=0):
        out = step(
            functools.partial(mix_kernel, len(pieces), place, splits),
            [struct((size, part), F32)] * count + [struct((size, count * part // splits), BF16)] * splits,
            a_own,
            a_other,
            *pieces,
            scratch=[held],
            work=work,
        )
        away = [swapped(other) for other in out[count:]]
        return [(own, away, j) for j, own in enumerate(out[:count])]

    def ring(terms, *arrived, work=0):
        own, away, j = terms
        return step(
            functools.partial(ring_kernel, j, len(away)), struct((size, part), BF16), own, *away, *arrived, work=work
        )

    def weights(blocks, shapes):
        return step(functools.partial(weight_kernel, blocks), shapes, a_own, a_other, g_own, g_other)

    def grad_of(pieces, top, *earlier):
        here = sum(piece.shape[0] for piece in pieces)
        wide = here + sum(array.shape[1] for array in earlier[:1])
        return step(
            functools.partial(grad_kernel, top, len(pieces), len(earlier)),
            [struct((size, wide), BF16)] * 2,
            g_own,
            g_other,
            first,
            *pieces,
            *earlier,
            scratch=[pltpu.VMEM((here, width), BF16)],
        )

    if four:
        small = lambda dtype: struct((rows, middle), dtype)
        blocks = [
            (3, 0, middle), (3, middle, width), (2, 0, middle), (1, middle, width), (1, 0, middle), (2, middle, width), (0, 0, width),
        ]
        *far, mid_left, mid_right, near_left, near_right, own_sum = weights(
            blocks, [small(BF16)] * 2 + [small(F32)] * 2 + [small(BF16)] * 2 + [struct((rows, width), F32)]
        )
    terms = mix([first], 0, near_heads, 3 if four else 1)
    arrived = passed(ring(terms[0]))
    if four:
        rest_one, rest_two = flipped(w_again, 1), flipped(w_again, 2)
        on_one, on_two = step(rows_kernel, [lower(w_rest)] * 2, rest_one, rest_two)
        rest = [w_rest, rest_one, rest_two, flipped(on_one, 2), flipped(on_two, 1)]
        far_left, far_right = flipped(far[0], 1), flipped(far[1], 2)
        grad_own, grad_away = grad_of(rest[3:], 3 * rows, *grad_of(rest[:3], 0))
    else:
        grad_own, grad_away = grad_of(rest, 0)
    grad_other = swapped(grad_away)
    for j in range(1, near_heads):
        arrived = passed(ring(terms[j], arrived, work=C17))
    grad, back = step(
        functools.partial(back_contrib_kernel, groups),
        (flat(BF16), state_shape),
        grad_own,
        grad_other,
        pick_own,
        pick_other,
        q,
        row,
        col,
    )
    if four:
        near = flipped(back, 1)
    else:
        after = hops_of(back, False)
    if four:
        to_left, to_right = step(onward_kernel, [small(BF16)] * 2, mid_left, mid_right, far_left, far_right)
        on_right = flipped(to_right, 1)
        near_right = flipped(near_right, 2)
    terms = mix(rest, 0, 1)
    if four:
        pair, near_left, to_left = step(
            functools.partial(back_pair_kernel, groups),
            [struct((features, DH), BF16), small(BF16), small(BF16)],
            back,
            near,
            near_left,
            to_left,
            work=C20,
        )
        after = [near, lax.ppermute(pair, "ctx", [(2, 0), (3, 1)])]
        near_left, on_left = flipped(near_left, 1), flipped(to_left, 2)
    query_grad, key_part, value_part = step(
        functools.partial(back_intra_kernel, groups),
        (flat(BF16), flat(F32), flat(F32)),
        grad,
        q,
        k,
        v,
        row,
        col,
        low,
    )
    for j in range(1, heads - near_heads):
        arrived = passed(ring(terms[0], arrived))
        terms = mix(rest, j, 1)
    if four:
        own_sum = step(functools.partial(total_kernel, (1, 1)), struct((rows, width), F32), own_sum, near_right, on_right)
    key_grad, value_grad = step(
        functools.partial(back_inter_kernel, groups, len(after)),
        (flat(BF16), flat(BF16)),
        *after,
        k,
        v,
        col,
        key_part,
        value_part,
        work=C24,
    )
    mixed = ring(terms[0], arrived, work=C26)
    if four:
        w_grad = step(functools.partial(total_kernel, (0, 0)), struct((rows, width), F32), own_sum, near_left, on_left)
    else:
        w_grad = contract(a_own, g, 0, 0) + contract(a_other, g_other, 0, 0)
        w_grad = lax.psum_scatter(w_grad.astype(BF16), "ctx", scatter_dimension=0, tiled=True).astype(F32)
    return (
        mixed[None],
        query_grad[None],
        key_grad[None],
        value_grad[None],
        w_grad.reshape(rows_each, groups, width),
    )


def solution(mesh):
    return jax.shard_map(
        shards,
        mesh=mesh,
        in_specs=(
            P("dp", "ctx", "head"),
            P("dp", "ctx", "head"),
            P("dp", "ctx", "head"),
            P("dp", "head", "ctx"),
            P(("ctx", "dp"), "head", None),
            P("dp", "ctx", None),
        ),
        out_specs=(
            P("dp", "ctx", "head"),
            P("dp", "ctx", "head"),
            P("dp", "ctx", "head"),
            P("dp", "ctx", "head"),
            P(("ctx", "dp"), "head", None),
        ),
        check_vma=False,
    )
```

```python
import functools

import jax
import jax.numpy as jnp
from jax import lax
from jax.experimental import pallas as pl
from jax.experimental.pallas import tpu as pltpu
from jax.sharding import PartitionSpec as P

DH = 128
SCALE = 1.0 / DH
F32 = jnp.float32
BF16 = jnp.bfloat16
EXTRA = 16
C_JOIN, C26, C17, C20, C24 = 1070000000, 642000000, 1284000000, 642000000, 2140000000


def contract(a, b, dim_a, dim_b):
    return lax.dot_general(a, b, (((dim_a,), (dim_b,)), ((), ())), preferred_element_type=F32)


def head(ref, h):
    return ref[:, h * DH : (h + 1) * DH]


def call(kernel, out_shape, *args, staged=(), free_in=(), scratch=(), after=(), room=24, work=0):
    outs = list(out_shape) if isinstance(out_shape, (list, tuple)) else [out_shape]
    n, waits, count, made = len(args), len(after), len(staged), len(outs)

    def body(*refs):
        ins, rest = list(refs[:n]), refs[n + waits :]
        results, rest = rest[: made + 1], rest[made + 1 :]
        rest, buffers, sem = rest[: len(rest) - count - 1], rest[len(rest) - count - 1 : -1], rest[-1]
        copies = [pltpu.make_async_copy(ins[i], buffers[j], sem.at[j]) for j, i in enumerate(staged)]
        for copy in copies:
            copy.start()
        results[-1][...] = jnp.zeros_like(results[-1])
        for copy in copies:
            copy.wait()
        for j, i in enumerate(staged):
            ins[i] = buffers[j]
        kernel(*ins, *results[:-1], *rest)

    anywhere, local, far = (pl.BlockSpec(memory_space=m) for m in (pl.ANY, pltpu.VMEM, pltpu.HBM))
    results = pl.pallas_call(
        body,
        name=getattr(kernel, "func", kernel).__name__,
        out_shape=[*outs, struct((8, 128), F32)],
        in_specs=[far if i in staged or i in free_in else local for i in range(n)] + [anywhere] * waits,
        out_specs=[local] * (made + 1),
        scratch_shapes=[
            *scratch,
            *[pltpu.VMEM(args[i].shape, args[i].dtype) for i in staged],
            pltpu.SemaphoreType.DMA((max(count, 1),)),
        ],
        compiler_params=pltpu.CompilerParams(vmem_limit_bytes=room * 1024 * 1024),
        cost_estimate=pl.CostEstimate(flops=work, bytes_accessed=0, transcendentals=0),
    )(*args, *after)
    return (results[:-1] if isinstance(out_shape, (list, tuple)) else results[0]), results[-1]


def struct(shape, dtype):
    return jax.ShapeDtypeStruct(shape, dtype)


def store_decay(out_ref, row, groups):
    decay = jnp.broadcast_to(jnp.exp(row[:, -1:]), (groups, DH))
    high = decay.astype(BF16).astype(F32)
    both = jnp.concatenate([high, decay - high], axis=0)
    out_ref[groups * DH : groups * DH + EXTRA, :] = both.astype(BF16)


def load_decay(ref, groups):
    both = ref[groups * DH : groups * DH + EXTRA, :].astype(F32)
    return both[:groups] + both[groups:]


def entering(refs, groups, forward):
    if lax.axis_size("ctx") == 4:
        near, far = refs
        bit = side(forward)
        decay = load_decay(near, groups) * bit + (1.0 - bit)
        return lambda h: rows_of(near, h) * bit + decay[h : h + 1, :] * rows_of(far, h)
    decays = [load_decay(ref, groups) for ref in refs[:-1]]

    def state(h):
        total = rows_of(refs[-1], h)
        for ref, decay in zip(refs[-2::-1], decays[::-1]):
            total = rows_of(ref, h) + decay[h : h + 1, :] * total
        return total

    return state


def rows_of(ref, h):
    return ref[h * DH : (h + 1) * DH, :].astype(F32)


def side(forward):
    bit = lax.rem(lax.axis_index("ctx"), 2).astype(F32)
    return bit if forward else 1.0 - bit


def pair_kernel(groups, forward, own_ref, near_ref, *refs):
    out_ref = refs[-1]
    if len(refs) == 3:
        refs[1][...] = refs[0][...]
    bit = side(forward)
    own_decay, near_decay = load_decay(own_ref, groups), load_decay(near_ref, groups)
    for h in range(groups):
        here = slice(h, h + 1)
        own, near = rows_of(own_ref, h), rows_of(near_ref, h)
        own_share = bit + (1.0 - bit) * near_decay[here]
        near_share = bit * own_decay[here] + (1.0 - bit)
        out_ref[h * DH : (h + 1) * DH, :] = (own_share * own + near_share * near).astype(BF16)


def lower_mask(size):
    return lax.broadcasted_iota(jnp.int32, (size, size), 0) >= lax.broadcasted_iota(
        jnp.int32, (size, size), 1
    )


def ring_columns(w_ref, out_ref, hops, sem):
    width = w_ref.shape[1] // lax.axis_size("head")
    copies = []
    for j in range(out_ref.shape[1] // width):
        here = pl.ds(j * width, width)
        copies.append(pltpu.make_async_copy(w_ref.at[:, columns_after(hops + j, width)], out_ref.at[:, here], sem.at[j]))
        copies[-1].start()
    return copies


def columns_kernel(w_ref, first_ref, rest_ref, sem):
    count = first_ref.shape[1] * lax.axis_size("head") // w_ref.shape[1]
    copies = ring_columns(w_ref, first_ref, 1, sem)
    copies += ring_columns(w_ref, rest_ref, 1 + count, sem.at[pl.ds(count, sem.shape[0] - count)])
    for copy in copies:
        copy.wait()


def sums(ld_ref, mask, rows):
    lower = mask.astype(F32)
    a, b = (lower, ld_ref[...]) if rows else (ld_ref[...], lower)
    return lax.dot_general(
        a, b, (((1,), (1,)), ((), ())), precision=lax.Precision.HIGHEST, preferred_element_type=F32
    )


def contrib_kernel(groups, k_ref, v_ref, ld_ref, state_ref):
    size = k_ref.shape[0]
    mask = lower_mask(size)
    col = sums(ld_ref, mask, True)
    tail = jnp.exp(col[size - 1 :, :] - col)
    for h in range(groups):
        weighted = (head(k_ref, h).astype(F32) * tail[:, h : h + 1]).astype(BF16)
        state_ref[h * DH : (h + 1) * DH, :] = contract(weighted, head(v_ref, h), 0, 0).astype(BF16)
    store_decay(state_ref, sums(ld_ref, mask, False), groups)


def intra_kernel(groups, q_ref, k_ref, v_ref, ld_ref, row_ref, col_ref, intra_ref):
    mask = lower_mask(q_ref.shape[0])
    row_ref[...] = sums(ld_ref, mask, False)
    col_ref[...] = sums(ld_ref, mask, True)
    for h in range(groups):
        probs = probs_of(q_ref, k_ref, spread_weights(row_ref, col_ref, mask, h), h)
        intra_ref[:, h * DH : (h + 1) * DH] = contract(probs, head(v_ref, h), 1, 0)


def probs_of(q_ref, k_ref, weights, h):
    return (contract(head(q_ref, h), head(k_ref, h), 1, 1) * SCALE * weights).astype(BF16)


def spread_weights(row_ref, col_ref, lower, h):
    spread = col_ref[:, h : h + 1] - row_ref[h : h + 1, :]
    return jnp.exp(jnp.where(lower, spread, -jnp.inf))


def attended_kernel(groups, count, *refs):
    states = refs[:count]
    q_ref, intra_ref, col_ref, pick_own_ref, pick_other_ref, g_ref = refs[count : count + 6]
    own_ref, other_ref, low_ref, held_ref, attended_ref, sem = refs[count + 6 :]
    copy = pltpu.make_async_copy(g_ref, held_ref, sem.at[0])
    copy.start()
    state = entering(states, groups, True)
    factor = jnp.exp(col_ref[...]) * SCALE
    for h in range(groups):
        low = state(h).astype(BF16)
        low_ref[h] = low
        inter = contract(head(q_ref, h), low, 1, 0)
        attended_ref[:, h * DH : (h + 1) * DH] = (
            head(intra_ref, h) + inter * factor[:, h : h + 1]
        ).astype(BF16)
    own_ref[...] = contract(attended_ref[...], pick_own_ref[...], 1, 0).astype(BF16)
    other_ref[...] = contract(attended_ref[...], pick_other_ref[...], 1, 0).astype(BF16)
    copy.wait()


def back_contrib_kernel(
    groups, own_ref, other_ref, pick_own_ref, pick_other_ref, q_ref, row_ref, col_ref, grad_ref, state_ref
):
    grad_ref[...] = (
        contract(own_ref[...], pick_own_ref[...], 1, 1) + contract(other_ref[...], pick_other_ref[...], 1, 1)
    ).astype(BF16)
    factor = jnp.exp(col_ref[...]) * SCALE
    for h in range(groups):
        weighted = (head(q_ref, h).astype(F32) * factor[:, h : h + 1]).astype(BF16)
        state_ref[h * DH : (h + 1) * DH, :] = contract(weighted, head(grad_ref, h), 0, 0).astype(BF16)
    store_decay(state_ref, row_ref[...], groups)


def back_key_kernel(groups, grad_ref, q_ref, v_ref, row_ref, col_ref, dprobs_ref, kpart_ref):
    lower = lower_mask(q_ref.shape[0])
    for h in range(groups):
        weights = spread_weights(row_ref, col_ref, lower, h)
        dprobs = (contract(head(grad_ref, h), head(v_ref, h), 1, 1) * SCALE * weights).astype(BF16)
        dprobs_ref[h] = dprobs
        kpart_ref[:, h * DH : (h + 1) * DH] = contract(dprobs, head(q_ref, h), 0, 0)


def back_query_kernel(groups, grad_ref, q_ref, k_ref, row_ref, col_ref, low_ref, dprobs_ref, qgrad_ref, vpart_ref):
    lower = lower_mask(q_ref.shape[0])
    factor = jnp.exp(col_ref[...]) * SCALE
    for h in range(groups):
        here = slice(h * DH, (h + 1) * DH)
        grad = head(grad_ref, h)
        qgrad_ref[:, here] = (
            contract(dprobs_ref[h], head(k_ref, h), 1, 0)
            + contract(grad, low_ref[h], 1, 1) * factor[:, h : h + 1]
        ).astype(BF16)
        probs = probs_of(q_ref, k_ref, spread_weights(row_ref, col_ref, lower, h), h)
        vpart_ref[:, here] = contract(probs, grad, 0, 0)


def back_inter_kernel(groups, count, *refs):
    states = refs[:count]
    k_ref, v_ref, col_ref, kpart_ref, vpart_ref, kgrad_ref, vgrad_ref = refs[count:]
    state = entering(states, groups, False)
    col = col_ref[...]
    tail = jnp.exp(col[col.shape[0] - 1 :, :] - col)
    for h in range(groups):
        here = slice(h * DH, (h + 1) * DH)
        low = state(h).astype(BF16)
        kgrad_ref[:, here] = (
            head(kpart_ref, h) + tail[:, h : h + 1] * contract(head(v_ref, h), low, 1, 1)
        ).astype(BF16)
        vgrad_ref[:, here] = (
            head(vpart_ref, h) + tail[:, h : h + 1] * contract(head(k_ref, h), low, 1, 0)
        ).astype(BF16)


def hops_of(state, forward):
    devices = lax.axis_size("ctx")
    out = []
    for hop in range(1, devices):
        if forward:
            pairs = [(i, i + hop) for i in range(devices - hop)]
        else:
            pairs = [(i + hop, i) for i in range(devices - hop)]
        out.append(lax.ppermute(state, "ctx", pairs))
    return out


def swapped(array):
    return lax.ppermute(array, "dp", [(0, 1), (1, 0)])


def flipped(array, bit):
    return lax.ppermute(array, "ctx", [(i, i ^ bit) for i in range(4)])


def pass_kernel(one, two, whole, on_one, on_two, again):
    again[...] = whole[...]
    rows_kernel(one, two, on_one, on_two)


def rows_kernel(one, two, on_one, on_two):
    half = on_one.shape[0]
    on_one[...] = one[:half]
    on_two[...] = two[half:]


def join_kernel(*refs):
    lay_out(refs[:-1], refs[-1])


def lay_out(pieces, out_ref, columns=slice(None)):
    top = 0
    for piece in pieces:
        out_ref[top : top + piece.shape[0], :] = piece[:, columns]
        top += piece.shape[0]


def along(place):
    return place ^ (place >> 1) if lax.axis_size("head") == 4 else place


def columns_after(hops, width):
    devices = lax.axis_size("head")
    device = along(lax.rem(along(lax.axis_index("head")) + hops, devices))
    return pl.ds(pl.multiple_of(device * width, width), width)


def mix_kernel(count, place, splits, a_own, a_other, *refs):
    pieces, owns, others, w_ref = refs[:count], refs[count : -1 - splits], refs[-1 - splits : -1], refs[-1]
    width = w_ref.shape[1]
    away = []
    for j, own in enumerate(owns):
        lay_out(pieces, w_ref, slice((place + j) * width, (place + j + 1) * width))
        own[...] = contract(a_own[...], w_ref[...], 1, 0)
        away.append(contract(a_other[...], w_ref[...], 1, 0).astype(BF16))
    away = away[0] if len(away) == 1 else jnp.concatenate(away, axis=1)
    for i, other in enumerate(others):
        other[...] = away[:, i * other.shape[1] : (i + 1) * other.shape[1]]


def grad_kernel(top, count, earlier, g_own, g_other, first_ref, *refs):
    pieces, before, (own, other, w_ref) = refs[:count], refs[count : count + earlier], refs[count + earlier :]
    heads = lax.axis_size("head")
    rows, left, width = w_ref.shape[0], first_ref.shape[1], w_ref.shape[1] // heads
    w_ref[:, :left] = first_ref[top : top + rows]
    lay_out(pieces, w_ref.at[:, left:])
    for g_ref, old, out in ((g_own, before[:1], own), (g_other, before[1:], other)):
        total = None
        for j in range(heads):
            term = contract(
                g_ref[:, columns_after(1 + j, width)], w_ref[:, j * width : (j + 1) * width], 1, 1
            )
            total = term if total is None else total + term
        start = out.shape[1] - rows
        if old:
            out[:, :start] = old[0][...]
        out[:, start:] = total.astype(BF16)


def weight_kernel(blocks, a_own, a_other, g_own, g_other, *outs):
    rows = a_own.shape[1] // 4
    for stack, out in zip(blocks, outs):
        for i, (k, left, right) in enumerate(stack):
            here = slice(k * rows, (k + 1) * rows)
            out[i * rows : (i + 1) * rows] = (
                contract(a_own[:, here], g_own[:, left:right], 0, 0)
                + contract(a_other[:, here], g_other[:, left:right], 0, 0)
            ).astype(out.dtype)


def onward_kernel(mid_ref, far_ref, out_ref):
    out_ref[...] = (mid_ref[...] + far_ref[: mid_ref.shape[0]].astype(F32)).astype(BF16)


def total_kernel(own_ref, left_ref, right_ref, out_ref):
    rows, half = own_ref.shape[0], own_ref.shape[1] // 2
    for here, ref in ((slice(0, half), left_ref), (slice(half, 2 * half), right_ref)):
        out_ref[:, here] = own_ref[:, here] + ref[ref.shape[0] - rows :].astype(F32)


def ring_kernel(j, count, own_ref, *refs):
    width = own_ref.shape[1]
    other = [ref[...] for ref in refs[:count]]
    other = other[0] if count == 1 else jnp.concatenate(other, axis=1)
    total = own_ref[...] + other[:, j * width : (j + 1) * width].astype(F32)
    if len(refs) == count + 2:
        total = total + refs[count][...].astype(F32)
    refs[-1][...] = total.astype(BF16)


def passed(array):
    devices = lax.axis_size("head")
    pairs = [(along(i), along((i - 1) % devices)) for i in range(devices)]
    return lax.ppermute(array, "head", pairs)


def picks_kernel(groups, rows_each, own_ref, other_ref):
    devices, mine, core = lax.axis_size("ctx"), lax.axis_index("ctx"), lax.axis_index("dp")
    width = own_ref.shape[1]
    shape = (DH, width)
    feature, place = lax.broadcasted_iota(jnp.int32, shape, 0), lax.broadcasted_iota(jnp.int32, shape, 1)
    block = place // (rows_each * groups)
    if devices == 4:
        block = block ^ mine
    row = (place // groups) % rows_each
    for p, ref in ((core, own_ref), (1 - core, other_ref)):
        match = feature == (block * 2 + p) * rows_each + row
        for h in range(groups):
            ref[h * DH : (h + 1) * DH, :] = (match & (place % groups == h)).astype(F32).astype(BF16)


def shards(queries, keys, values, log_decay, w_out, grad_out):
    groups = log_decay.shape[1]
    size = queries.shape[1]
    devices, heads = lax.axis_size("ctx"), lax.axis_size("head")
    four = devices == 4
    q, k, v, ld, g = queries[0], keys[0], values[0], log_decay[0], grad_out[0]
    rows_each, _, width = w_out.shape
    rows, part, middle = rows_each * groups, width // heads, width // 2
    w = w_out.reshape(rows, width)
    features = groups * DH
    state_shape = struct((features + EXTRA, DH), BF16)
    flat = lambda dtype: struct((size, features), dtype)
    half = struct((size, features // 2), BF16)
    last = []

    def step(kernel, out_shape, *args, after=(), **kwargs):
        out, done = call(kernel, out_shape, *args, after=[*last, *after], **kwargs)
        last[:] = [done]
        return out

    near_heads = heads // 2
    first_shape, rest_shape = (struct((rows, count * part), BF16) for count in (near_heads, heads - near_heads))
    state = step(
        functools.partial(contrib_kernel, groups), state_shape, k, v, ld, staged=(0, 1, 2), room=60
    )
    w_first, w_rest = step(
        columns_kernel,
        [first_shape, rest_shape],
        w,
        free_in=(0,),
        scratch=[pltpu.SemaphoreType.DMA((heads,))],
        room=60,
    )
    g_other = swapped(g)
    if four:
        near = flipped(state, 1)
        first_two, first_one = flipped(w_first, 2), flipped(w_first, 1)
        pair = step(functools.partial(pair_kernel, groups, True), struct((features, DH), BF16), state, near)
        before = [near, lax.ppermute(pair, "ctx", [(0, 2), (1, 3)])]
        lower = lambda array: struct((rows // 2, array.shape[1]), BF16)
    pick_own, pick_other = step(
        functools.partial(picks_kernel, groups, rows_each),
        [struct((features, features // 2), BF16)] * 2,
        after=[g_other],
    )
    row, col, intra = step(
        functools.partial(intra_kernel, groups),
        (struct((groups, size), F32), struct((size, groups), F32), flat(F32)),
        q,
        k,
        v,
        ld,
    )
    if four:
        on_one, on_two, w_again = step(
            pass_kernel, [lower(w_first)] * 2 + [rest_shape], first_one, first_two, w_rest
        )
        first = [w_first, first_one, first_two, flipped(on_one, 2), flipped(on_two, 1)]
    else:
        before = hops_of(state, True)
        first = lax.all_gather(w_first, "ctx", axis=0, tiled=True)
        rest = [lax.all_gather(w_rest, "ctx", axis=0, tiled=True)]
    a_own, a_away, low, g_own = step(
        functools.partial(attended_kernel, groups, len(before)),
        (half, half, struct((groups, DH, DH), BF16), struct(g.shape, BF16)),
        *before,
        q,
        intra,
        col,
        pick_own,
        pick_other,
        g,
        free_in=(len(before) + 5,),
        scratch=[pltpu.VMEM((size, features), BF16), pltpu.SemaphoreType.DMA((1,))],
    )
    a_other = swapped(a_away)
    if four:
        first = step(join_kernel, struct((devices * rows, first_shape.shape[1]), BF16), *first, work=C_JOIN)
    held = pltpu.VMEM((features // 2, part), BF16)

    def mix(pieces, place, count, splits=1, work=0):
        out = step(
            functools.partial(mix_kernel, len(pieces), place, splits),
            [struct((size, part), F32)] * count + [struct((size, count * part // splits), BF16)] * splits,
            a_own,
            a_other,
            *pieces,
            scratch=[held],
            work=work,
        )
        away = [swapped(other) for other in out[count:]]
        return [(own, away, j) for j, own in enumerate(out[:count])]

    def ring(terms, *arrived, work=0):
        own, away, j = terms
        return step(
            functools.partial(ring_kernel, j, len(away)), struct((size, part), BF16), own, *away, *arrived, work=work
        )

    def weights(blocks, shapes):
        return step(functools.partial(weight_kernel, blocks), shapes, a_own, a_other, g_own, g_other)

    def grad_of(pieces, top, *earlier):
        here = sum(piece.shape[0] for piece in pieces)
        wide = here + sum(array.shape[1] for array in earlier[:1])
        return step(
            functools.partial(grad_kernel, top, len(pieces), len(earlier)),
            [struct((size, wide), BF16)] * 2,
            g_own,
            g_other,
            first,
            *pieces,
            *earlier,
            scratch=[pltpu.VMEM((here, width), BF16)],
        )

    if four:
        small = lambda dtype: struct((rows, middle), dtype)
        left, right = (0, middle), (middle, width)
        blocks = [
            [(3, *left)], [(3, *right), (2, *right)], [(1, *left)], [(2, *left)], [(1, *right)], [(0, 0, width)],
        ]
        far_left, both_right, near_left, mid_left, mid_right, own_sum = weights(
            blocks,
            [small(BF16), struct((2 * rows, middle), BF16), small(BF16), small(F32), small(F32), struct((rows, width), F32)],
        )
    terms = mix([first], 0, near_heads, 3 if four else 1)
    arrived = passed(ring(terms[0]))
    if four:
        rest_one, rest_two = flipped(w_again, 1), flipped(w_again, 2)
        on_one, on_two = step(rows_kernel, [lower(w_rest)] * 2, rest_one, rest_two)
        rest = [w_rest, rest_one, rest_two, flipped(on_one, 2), flipped(on_two, 1)]
        far_left, both_right, near_left = flipped(far_left, 1), flipped(both_right, 2), flipped(near_left, 1)
        grad_own, grad_away = grad_of(rest[3:], 3 * rows, *grad_of(rest[:3], 0))
    else:
        grad_own, grad_away = grad_of(rest, 0)
    grad_other = swapped(grad_away)
    for j in range(1, near_heads):
        arrived = passed(ring(terms[j], arrived, work=C17))
    grad, back = step(
        functools.partial(back_contrib_kernel, groups),
        (flat(BF16), state_shape),
        grad_own,
        grad_other,
        pick_own,
        pick_other,
        q,
        row,
        col,
    )
    if four:
        near = flipped(back, 1)
    else:
        after = hops_of(back, False)
    if four:
        on_left = flipped(step(onward_kernel, small(BF16), mid_left, far_left), 2)
    terms = mix(rest, 0, 1)
    if four:
        pair = step(
            functools.partial(pair_kernel, groups, False), struct((features, DH), BF16), back, near, work=C20
        )
        after = [near, lax.ppermute(pair, "ctx", [(2, 0), (3, 1)])]
    dprobs, key_part = step(
        functools.partial(back_key_kernel, groups),
        (struct((groups, size, size), BF16), flat(F32)),
        grad,
        q,
        v,
        row,
        col,
    )
    for j in range(1, heads - near_heads):
        arrived = passed(ring(terms[0], arrived))
        if four and j == 1:
            on_right = flipped(step(onward_kernel, small(BF16), mid_right, both_right), 1)
        if j == 1:
            query_grad, value_part = step(
                functools.partial(back_query_kernel, groups),
                (flat(BF16), flat(F32)),
                grad,
                q,
                k,
                row,
                col,
                low,
                dprobs,
            )
        terms = mix(rest, j, 1, 2 if four else 1)
    if four:
        own_sum = step(total_kernel, struct((rows, width), F32), own_sum, near_left, both_right)
    key_grad, value_grad = step(
        functools.partial(back_inter_kernel, groups, len(after)),
        (flat(BF16), flat(BF16)),
        *after,
        k,
        v,
        col,
        key_part,
        value_part,
        work=C24,
    )
    mixed = ring(terms[0], arrived, work=C26)
    if four:
        w_grad = step(total_kernel, struct((rows, width), F32), own_sum, on_left, on_right)
    else:
        w_grad = contract(a_own, g, 0, 0) + contract(a_other, g_other, 0, 0)
        w_grad = lax.psum_scatter(w_grad.astype(BF16), "ctx", scatter_dimension=0, tiled=True).astype(F32)
    return (
        mixed[None],
        query_grad[None],
        key_grad[None],
        value_grad[None],
        w_grad.reshape(rows_each, groups, width),
    )


def solution(mesh):
    return jax.shard_map(
        shards,
        mesh=mesh,
        in_specs=(
            P("dp", "ctx", "head"),
            P("dp", "ctx", "head"),
            P("dp", "ctx", "head"),
            P("dp", "head", "ctx"),
            P(("ctx", "dp"), "head", None),
            P("dp", "ctx", None),
        ),
        out_specs=(
            P("dp", "ctx", "head"),
            P("dp", "ctx", "head"),
            P("dp", "ctx", "head"),
            P("dp", "ctx", "head"),
            P(("ctx", "dp"), "head", None),
        ),
        check_vma=False,
    )
```

```python
import functools

import jax
import jax.numpy as jnp
from jax import lax
from jax.experimental import pallas as pl
from jax.experimental.pallas import tpu as pltpu
from jax.sharding import PartitionSpec as P

DH = 128
SCALE = 1.0 / DH
F32 = jnp.float32
BF16 = jnp.bfloat16
EXTRA = 16
C_HOLD, C_JOIN, C26, C17, C20, C24 = 1070000000, 1070000000, 642000000, 1284000000, 642000000, 2140000000


def contract(a, b, dim_a, dim_b):
    return lax.dot_general(a, b, (((dim_a,), (dim_b,)), ((), ())), preferred_element_type=F32)


def head(ref, h):
    return ref[:, h * DH : (h + 1) * DH]


def call(kernel, out_shape, *args, staged=(), free_in=(), scratch=(), after=(), room=24, work=0):
    outs = list(out_shape) if isinstance(out_shape, (list, tuple)) else [out_shape]
    n, waits, count, made = len(args), len(after), len(staged), len(outs)

    def body(*refs):
        ins, rest = list(refs[:n]), refs[n + waits :]
        results, rest = rest[: made + 1], rest[made + 1 :]
        rest, buffers, sem = rest[: len(rest) - count - 1], rest[len(rest) - count - 1 : -1], rest[-1]
        copies = [pltpu.make_async_copy(ins[i], buffers[j], sem.at[j]) for j, i in enumerate(staged)]
        for copy in copies:
            copy.start()
        results[-1][...] = jnp.zeros_like(results[-1])
        for copy in copies:
            copy.wait()
        for j, i in enumerate(staged):
            ins[i] = buffers[j]
        kernel(*ins, *results[:-1], *rest)

    anywhere, local, far = (pl.BlockSpec(memory_space=m) for m in (pl.ANY, pltpu.VMEM, pltpu.HBM))
    results = pl.pallas_call(
        body,
        name=getattr(kernel, "func", kernel).__name__,
        out_shape=[*outs, struct((8, 128), F32)],
        in_specs=[far if i in staged or i in free_in else local for i in range(n)] + [anywhere] * waits,
        out_specs=[local] * (made + 1),
        scratch_shapes=[
            *scratch,
            *[pltpu.VMEM(args[i].shape, args[i].dtype) for i in staged],
            pltpu.SemaphoreType.DMA((max(count, 1),)),
        ],
        compiler_params=pltpu.CompilerParams(vmem_limit_bytes=room * 1024 * 1024),
        cost_estimate=pl.CostEstimate(flops=work, bytes_accessed=0, transcendentals=0),
    )(*args, *after)
    return (results[:-1] if isinstance(out_shape, (list, tuple)) else results[0]), results[-1]


def struct(shape, dtype):
    return jax.ShapeDtypeStruct(shape, dtype)


def store_decay(out_ref, row, groups):
    decay = jnp.broadcast_to(jnp.exp(row[:, -1:]), (groups, DH))
    high = decay.astype(BF16).astype(F32)
    both = jnp.concatenate([high, decay - high], axis=0)
    out_ref[groups * DH : groups * DH + EXTRA, :] = both.astype(BF16)


def load_decay(ref, groups):
    both = ref[groups * DH : groups * DH + EXTRA, :].astype(F32)
    return both[:groups] + both[groups:]


def entering(refs, groups, forward):
    if lax.axis_size("ctx") == 4:
        near, far = refs
        bit = side(forward)
        decay = load_decay(near, groups) * bit + (1.0 - bit)
        return lambda h: rows_of(near, h) * bit + decay[h : h + 1, :] * rows_of(far, h)
    decays = [load_decay(ref, groups) for ref in refs[:-1]]

    def state(h):
        total = rows_of(refs[-1], h)
        for ref, decay in zip(refs[-2::-1], decays[::-1]):
            total = rows_of(ref, h) + decay[h : h + 1, :] * total
        return total

    return state


def rows_of(ref, h):
    return ref[h * DH : (h + 1) * DH, :].astype(F32)


def side(forward):
    bit = lax.rem(lax.axis_index("ctx"), 2).astype(F32)
    return bit if forward else 1.0 - bit


def pair_kernel(groups, forward, own_ref, near_ref, *refs):
    out_ref = refs[-1]
    if len(refs) == 3:
        refs[1][...] = refs[0][...]
    bit = side(forward)
    own_decay, near_decay = load_decay(own_ref, groups), load_decay(near_ref, groups)
    for h in range(groups):
        here = slice(h, h + 1)
        own, near = rows_of(own_ref, h), rows_of(near_ref, h)
        own_share = bit + (1.0 - bit) * near_decay[here]
        near_share = bit * own_decay[here] + (1.0 - bit)
        out_ref[h * DH : (h + 1) * DH, :] = (own_share * own + near_share * near).astype(BF16)


def lower_mask(size):
    return lax.broadcasted_iota(jnp.int32, (size, size), 0) >= lax.broadcasted_iota(
        jnp.int32, (size, size), 1
    )


def ring_columns(w_ref, out_ref, hops, sem):
    width = w_ref.shape[1] // lax.axis_size("head")
    copies = []
    for j in range(out_ref.shape[1] // width):
        here = pl.ds(j * width, width)
        copies.append(pltpu.make_async_copy(w_ref.at[:, columns_after(hops + j, width)], out_ref.at[:, here], sem.at[j]))
        copies[-1].start()
    return copies


def sums(ld_ref, mask, rows):
    lower = mask.astype(F32)
    a, b = (lower, ld_ref[...]) if rows else (ld_ref[...], lower)
    return lax.dot_general(
        a, b, (((1,), (1,)), ((), ())), precision=lax.Precision.HIGHEST, preferred_element_type=F32
    )


def contrib_kernel(groups, k_hbm, v_hbm, ld_hbm, w_ref, state_ref, first_ref, rest_ref, k_ref, v_ref, ld_ref, sem, w_sem):
    moves = [
        pltpu.make_async_copy(source, held, sem.at[i])
        for i, (source, held) in enumerate(((ld_hbm, ld_ref), (k_hbm, k_ref), (v_hbm, v_ref)))
    ]
    for move in moves:
        move.start()
    count = first_ref.shape[1] * lax.axis_size("head") // w_ref.shape[1]
    copies = ring_columns(w_ref, first_ref, 1, w_sem)
    copies += ring_columns(w_ref, rest_ref, 1 + count, w_sem.at[pl.ds(count, w_sem.shape[0] - count)])
    moves[0].wait()
    size = k_ref.shape[0]
    mask = lower_mask(size)
    col = sums(ld_ref, mask, True)
    tail = jnp.exp(col[size - 1 :, :] - col)
    store_decay(state_ref, sums(ld_ref, mask, False), groups)
    moves[1].wait()
    moves[2].wait()
    for h in range(groups):
        weighted = (head(k_ref, h).astype(F32) * tail[:, h : h + 1]).astype(BF16)
        state_ref[h * DH : (h + 1) * DH, :] = contract(weighted, head(v_ref, h), 0, 0).astype(BF16)
    for copy in copies:
        copy.wait()


def again_kernel(ref, again_ref):
    again_ref[...] = ref[...]


def intra_kernel(groups, q_ref, k_ref, v_ref, ld_ref, row_ref, col_ref, intra_ref):
    mask = lower_mask(q_ref.shape[0])
    row_ref[...] = sums(ld_ref, mask, False)
    col_ref[...] = sums(ld_ref, mask, True)
    for h in range(groups):
        probs = probs_of(q_ref, k_ref, spread_weights(row_ref, col_ref, mask, h), h)
        intra_ref[:, h * DH : (h + 1) * DH] = contract(probs, head(v_ref, h), 1, 0)


def probs_of(q_ref, k_ref, weights, h):
    return (contract(head(q_ref, h), head(k_ref, h), 1, 1) * SCALE * weights).astype(BF16)


def spread_weights(row_ref, col_ref, lower, h):
    spread = col_ref[:, h : h + 1] - row_ref[h : h + 1, :]
    return jnp.exp(jnp.where(lower, spread, -jnp.inf))


def attended_kernel(groups, count, *refs):
    states = refs[:count]
    q_ref, intra_ref, col_ref, pick_own_ref, pick_other_ref, g_ref = refs[count : count + 6]
    own_ref, other_ref, low_ref, held_ref, attended_ref, sem = refs[count + 6 :]
    copy = pltpu.make_async_copy(g_ref, held_ref, sem.at[0])
    copy.start()
    state = entering(states, groups, True)
    factor = jnp.exp(col_ref[...]) * SCALE
    for h in range(groups):
        low = state(h).astype(BF16)
        low_ref[h] = low
        inter = contract(head(q_ref, h), low, 1, 0)
        attended_ref[:, h * DH : (h + 1) * DH] = (
            head(intra_ref, h) + inter * factor[:, h : h + 1]
        ).astype(BF16)
    own_ref[...] = contract(attended_ref[...], pick_own_ref[...], 1, 0).astype(BF16)
    other_ref[...] = contract(attended_ref[...], pick_other_ref[...], 1, 0).astype(BF16)
    copy.wait()


def back_contrib_kernel(
    groups, own_ref, other_ref, pick_own_ref, pick_other_ref, q_ref, row_ref, col_ref, grad_ref, state_ref
):
    grad_ref[...] = (
        contract(own_ref[...], pick_own_ref[...], 1, 1) + contract(other_ref[...], pick_other_ref[...], 1, 1)
    ).astype(BF16)
    factor = jnp.exp(col_ref[...]) * SCALE
    for h in range(groups):
        weighted = (head(q_ref, h).astype(F32) * factor[:, h : h + 1]).astype(BF16)
        state_ref[h * DH : (h + 1) * DH, :] = contract(weighted, head(grad_ref, h), 0, 0).astype(BF16)
    store_decay(state_ref, row_ref[...], groups)


def back_key_kernel(groups, grad_ref, q_ref, v_ref, row_ref, col_ref, dprobs_ref, kpart_ref):
    lower = lower_mask(q_ref.shape[0])
    for h in range(groups):
        weights = spread_weights(row_ref, col_ref, lower, h)
        dprobs = (contract(head(grad_ref, h), head(v_ref, h), 1, 1) * SCALE * weights).astype(BF16)
        dprobs_ref[h] = dprobs
        kpart_ref[:, h * DH : (h + 1) * DH] = contract(dprobs, head(q_ref, h), 0, 0)


def back_query_kernel(groups, grad_ref, q_ref, k_ref, row_ref, col_ref, low_ref, dprobs_ref, qgrad_ref, vpart_ref):
    lower = lower_mask(q_ref.shape[0])
    factor = jnp.exp(col_ref[...]) * SCALE
    for h in range(groups):
        here = slice(h * DH, (h + 1) * DH)
        grad = head(grad_ref, h)
        qgrad_ref[:, here] = (
            contract(dprobs_ref[h], head(k_ref, h), 1, 0)
            + contract(grad, low_ref[h], 1, 1) * factor[:, h : h + 1]
        ).astype(BF16)
        probs = probs_of(q_ref, k_ref, spread_weights(row_ref, col_ref, lower, h), h)
        vpart_ref[:, here] = contract(probs, grad, 0, 0)


def back_inter_kernel(groups, count, *refs):
    states = refs[:count]
    k_ref, v_ref, col_ref, kpart_ref, vpart_ref, kgrad_ref, vgrad_ref = refs[count:]
    state = entering(states, groups, False)
    col = col_ref[...]
    tail = jnp.exp(col[col.shape[0] - 1 :, :] - col)
    for h in range(groups):
        here = slice(h * DH, (h + 1) * DH)
        low = state(h).astype(BF16)
        kgrad_ref[:, here] = (
            head(kpart_ref, h) + tail[:, h : h + 1] * contract(head(v_ref, h), low, 1, 1)
        ).astype(BF16)
        vgrad_ref[:, here] = (
            head(vpart_ref, h) + tail[:, h : h + 1] * contract(head(k_ref, h), low, 1, 0)
        ).astype(BF16)


def hops_of(state, forward):
    devices = lax.axis_size("ctx")
    out = []
    for hop in range(1, devices):
        if forward:
            pairs = [(i, i + hop) for i in range(devices - hop)]
        else:
            pairs = [(i + hop, i) for i in range(devices - hop)]
        out.append(lax.ppermute(state, "ctx", pairs))
    return out


def swapped(array):
    return lax.ppermute(array, "dp", [(0, 1), (1, 0)])


def flipped(array, bit):
    return lax.ppermute(array, "ctx", [(i, i ^ bit) for i in range(4)])


def rows_kernel(upper, ref, out_ref):
    half = out_ref.shape[0]
    out_ref[...] = ref[:half] if upper else ref[half:]


def join_kernel(*refs):
    lay_out(refs[:-1], refs[-1])


def lay_out(pieces, out_ref, columns=slice(None)):
    top = 0
    for piece in pieces:
        out_ref[top : top + piece.shape[0], :] = piece[:, columns]
        top += piece.shape[0]


def along(place):
    return place ^ (place >> 1) if lax.axis_size("head") == 4 else place


def columns_after(hops, width):
    devices = lax.axis_size("head")
    device = along(lax.rem(along(lax.axis_index("head")) + hops, devices))
    return pl.ds(pl.multiple_of(device * width, width), width)


def mix_kernel(count, place, splits, a_own, a_other, *refs):
    pieces, owns, others, w_ref = refs[:count], refs[count : -1 - splits], refs[-1 - splits : -1], refs[-1]
    width = w_ref.shape[1]
    away = []
    for j, own in enumerate(owns):
        lay_out(pieces, w_ref, slice((place + j) * width, (place + j + 1) * width))
        own[...] = contract(a_own[...], w_ref[...], 1, 0)
        away.append(contract(a_other[...], w_ref[...], 1, 0).astype(BF16))
    away = away[0] if len(away) == 1 else jnp.concatenate(away, axis=1)
    for i, other in enumerate(others):
        other[...] = away[:, i * other.shape[1] : (i + 1) * other.shape[1]]


def grad_kernel(top, count, earlier, g_own, g_other, first_ref, *refs):
    pieces, before, (own, other, w_ref) = refs[:count], refs[count : count + earlier], refs[count + earlier :]
    heads = lax.axis_size("head")
    rows, left, width = w_ref.shape[0], first_ref.shape[1], w_ref.shape[1] // heads
    w_ref[:, :left] = first_ref[top : top + rows]
    lay_out(pieces, w_ref.at[:, left:])
    for g_ref, old, out in ((g_own, before[:1], own), (g_other, before[1:], other)):
        total = None
        for j in range(heads):
            term = contract(
                g_ref[:, columns_after(1 + j, width)], w_ref[:, j * width : (j + 1) * width], 1, 1
            )
            total = term if total is None else total + term
        start = out.shape[1] - rows
        if old:
            out[:, :start] = old[0][...]
        out[:, start:] = total.astype(BF16)


def weight_kernel(blocks, a_own, a_other, g_own, g_other, *outs):
    rows = a_own.shape[1] // 4
    for stack, out in zip(blocks, outs):
        for i, (k, left, right) in enumerate(stack):
            here = slice(k * rows, (k + 1) * rows)
            out[i * rows : (i + 1) * rows] = (
                contract(a_own[:, here], g_own[:, left:right], 0, 0)
                + contract(a_other[:, here], g_other[:, left:right], 0, 0)
            ).astype(out.dtype)


def onward_kernel(mid_ref, far_ref, out_ref):
    out_ref[...] = (mid_ref[...] + far_ref[: mid_ref.shape[0]].astype(F32)).astype(BF16)


def total_kernel(own_ref, left_ref, right_ref, out_ref):
    rows, half = own_ref.shape[0], own_ref.shape[1] // 2
    for here, ref in ((slice(0, half), left_ref), (slice(half, 2 * half), right_ref)):
        out_ref[:, here] = own_ref[:, here] + ref[ref.shape[0] - rows :].astype(F32)


def ring_kernel(j, count, own_ref, *refs):
    width = own_ref.shape[1]
    other = [ref[...] for ref in refs[:count]]
    other = other[0] if count == 1 else jnp.concatenate(other, axis=1)
    total = own_ref[...] + other[:, j * width : (j + 1) * width].astype(F32)
    if len(refs) == count + 2:
        total = total + refs[count][...].astype(F32)
    refs[-1][...] = total.astype(BF16)


def passed(array):
    devices = lax.axis_size("head")
    pairs = [(along(i), along((i - 1) % devices)) for i in range(devices)]
    return lax.ppermute(array, "head", pairs)


def picks_kernel(groups, rows_each, own_ref, other_ref):
    devices, mine, core = lax.axis_size("ctx"), lax.axis_index("ctx"), lax.axis_index("dp")
    width = own_ref.shape[1]
    shape = (DH, width)
    feature, place = lax.broadcasted_iota(jnp.int32, shape, 0), lax.broadcasted_iota(jnp.int32, shape, 1)
    block = place // (rows_each * groups)
    if devices == 4:
        block = block ^ mine
    row = (place // groups) % rows_each
    for p, ref in ((core, own_ref), (1 - core, other_ref)):
        match = feature == (block * 2 + p) * rows_each + row
        for h in range(groups):
            ref[h * DH : (h + 1) * DH, :] = (match & (place % groups == h)).astype(F32).astype(BF16)


def shards(queries, keys, values, log_decay, w_out, grad_out):
    groups = log_decay.shape[1]
    size = queries.shape[1]
    devices, heads = lax.axis_size("ctx"), lax.axis_size("head")
    four = devices == 4
    q, k, v, ld, g = queries[0], keys[0], values[0], log_decay[0], grad_out[0]
    rows_each, _, width = w_out.shape
    rows, part, middle = rows_each * groups, width // heads, width // 2
    w = w_out.reshape(rows, width)
    features = groups * DH
    state_shape = struct((features + EXTRA, DH), BF16)
    flat = lambda dtype: struct((size, features), dtype)
    half = struct((size, features // 2), BF16)
    last = []

    def step(kernel, out_shape, *args, after=(), **kwargs):
        out, done = call(kernel, out_shape, *args, after=[*last, *after], **kwargs)
        last[:] = [done]
        return out

    near_heads = heads // 2
    first_shape, rest_shape = (struct((rows, count * part), BF16) for count in (near_heads, heads - near_heads))
    state, w_first, w_rest = step(
        functools.partial(contrib_kernel, groups),
        [state_shape, first_shape, rest_shape],
        k,
        v,
        ld,
        w,
        free_in=(0, 1, 2, 3),
        scratch=[
            *[pltpu.VMEM(array.shape, array.dtype) for array in (k, v, ld)],
            pltpu.SemaphoreType.DMA((3,)),
            pltpu.SemaphoreType.DMA((heads,)),
        ],
        room=60,
    )
    g_other = swapped(g)
    if four:
        near = flipped(state, 1)
        first_two, first_one = flipped(w_first, 2), flipped(w_first, 1)
        state = step(again_kernel, state_shape, state)
        pair = step(functools.partial(pair_kernel, groups, True), struct((features, DH), BF16), state, near)
        before = [near, lax.ppermute(pair, "ctx", [(0, 2), (1, 3)])]
        lower = lambda array: struct((rows // 2, array.shape[1]), BF16)
    pick_own, pick_other = step(
        functools.partial(picks_kernel, groups, rows_each),
        [struct((features, features // 2), BF16)] * 2,
        after=[g_other],
    )
    row, col, intra = step(
        functools.partial(intra_kernel, groups),
        (struct((groups, size), F32), struct((size, groups), F32), flat(F32)),
        q,
        k,
        v,
        ld,
    )
    if four:
        on_two = step(functools.partial(rows_kernel, True), lower(w_first), first_two)
        on_one = step(functools.partial(rows_kernel, False), lower(w_first), first_one)
        w_again = step(again_kernel, rest_shape, w_rest)
        first = [w_first, first_one, first_two, flipped(on_two, 1), flipped(on_one, 2)]
    else:
        before = hops_of(state, True)
        first = lax.all_gather(w_first, "ctx", axis=0, tiled=True)
        rest = [lax.all_gather(w_rest, "ctx", axis=0, tiled=True)]
    a_own, a_away, low, g_own = step(
        functools.partial(attended_kernel, groups, len(before)),
        (half, half, struct((groups, DH, DH), BF16), struct(g.shape, BF16)),
        *before,
        q,
        intra,
        col,
        pick_own,
        pick_other,
        g,
        free_in=(len(before) + 5,),
        scratch=[pltpu.VMEM((size, features), BF16), pltpu.SemaphoreType.DMA((1,))],
    )
    a_other = swapped(a_away)
    if four:
        first[3] = step(again_kernel, lower(w_first), first[3], work=C_HOLD)
        first = step(join_kernel, struct((devices * rows, first_shape.shape[1]), BF16), *first, work=C_JOIN)
    held = pltpu.VMEM((features // 2, part), BF16)

    def mix(pieces, place, count, splits=1, work=0):
        out = step(
            functools.partial(mix_kernel, len(pieces), place, splits),
            [struct((size, part), F32)] * count + [struct((size, count * part // splits), BF16)] * splits,
            a_own,
            a_other,
            *pieces,
            scratch=[held],
            work=work,
        )
        away = [swapped(other) for other in out[count:]]
        return [(own, away, j) for j, own in enumerate(out[:count])]

    def ring(terms, *arrived, work=0):
        own, away, j = terms
        return step(
            functools.partial(ring_kernel, j, len(away)), struct((size, part), BF16), own, *away, *arrived, work=work
        )

    def weights(blocks, shapes):
        return step(functools.partial(weight_kernel, blocks), shapes, a_own, a_other, g_own, g_other)

    def grad_of(pieces, top, *earlier):
        here = sum(piece.shape[0] for piece in pieces)
        wide = here + sum(array.shape[1] for array in earlier[:1])
        return step(
            functools.partial(grad_kernel, top, len(pieces), len(earlier)),
            [struct((size, wide), BF16)] * 2,
            g_own,
            g_other,
            first,
            *pieces,
            *earlier,
            scratch=[pltpu.VMEM((here, width), BF16)],
        )

    terms = mix([first], 0, near_heads, 3 if four else 1)
    if four:
        small = lambda dtype: struct((rows, middle), dtype)
        left, right = (0, middle), (middle, width)
        blocks = [
            [(3, *left)], [(3, *right), (2, *right)], [(1, *left)], [(2, *left)], [(1, *right)], [(0, 0, width)],
        ]
        far_left, both_right, near_left, mid_left, mid_right, own_sum = weights(
            blocks,
            [small(BF16), struct((2 * rows, middle), BF16), small(BF16), small(F32), small(F32), struct((rows, width), F32)],
        )
    arrived = passed(ring(terms[0]))
    if four:
        rest_one, rest_two = flipped(w_again, 1), flipped(w_again, 2)
        on_two = step(functools.partial(rows_kernel, True), lower(w_rest), rest_two)
        on_one = step(functools.partial(rows_kernel, False), lower(w_rest), rest_one)
        rest = [w_rest, rest_one, rest_two, flipped(on_two, 1), flipped(on_one, 2)]
        far_left, both_right, near_left = flipped(far_left, 1), flipped(both_right, 2), flipped(near_left, 1)
        grad_own, grad_away = grad_of(rest[3:], 3 * rows, *grad_of(rest[:3], 0))
    else:
        grad_own, grad_away = grad_of(rest, 0)
    grad_other = swapped(grad_away)
    for j in range(1, near_heads):
        arrived = passed(ring(terms[j], arrived, work=C17))
    grad, back = step(
        functools.partial(back_contrib_kernel, groups),
        (flat(BF16), state_shape),
        grad_own,
        grad_other,
        pick_own,
        pick_other,
        q,
        row,
        col,
    )
    if four:
        near = flipped(back, 1)
    else:
        after = hops_of(back, False)
    if four:
        on_left = flipped(step(onward_kernel, small(BF16), mid_left, far_left), 2)
    terms = mix(rest, 0, 1)
    if four:
        pair = step(
            functools.partial(pair_kernel, groups, False), struct((features, DH), BF16), back, near, work=C20
        )
        after = [near, lax.ppermute(pair, "ctx", [(2, 0), (3, 1)])]
    dprobs, key_part = step(
        functools.partial(back_key_kernel, groups),
        (struct((groups, size, size), BF16), flat(F32)),
        grad,
        q,
        v,
        row,
        col,
    )
    for j in range(1, heads - near_heads):
        arrived = passed(ring(terms[0], arrived))
        if four and j == 1:
            on_right = flipped(step(onward_kernel, small(BF16), mid_right, both_right), 1)
        if j == 1:
            query_grad, value_part = step(
                functools.partial(back_query_kernel, groups),
                (flat(BF16), flat(F32)),
                grad,
                q,
                k,
                row,
                col,
                low,
                dprobs,
            )
        terms = mix(rest, j, 1, 2 if four else 1)
    if four:
        own_sum = step(total_kernel, struct((rows, width), F32), own_sum, near_left, both_right)
    key_grad, value_grad = step(
        functools.partial(back_inter_kernel, groups, len(after)),
        (flat(BF16), flat(BF16)),
        *after,
        k,
        v,
        col,
        key_part,
        value_part,
        work=C24,
    )
    mixed = ring(terms[0], arrived, work=C26)
    if four:
        w_grad = step(total_kernel, struct((rows, width), F32), own_sum, on_left, on_right)
    else:
        w_grad = contract(a_own, g, 0, 0) + contract(a_other, g_other, 0, 0)
        w_grad = lax.psum_scatter(w_grad.astype(BF16), "ctx", scatter_dimension=0, tiled=True).astype(F32)
    return (
        mixed[None],
        query_grad[None],
        key_grad[None],
        value_grad[None],
        w_grad.reshape(rows_each, groups, width),
    )


def solution(mesh):
    return jax.shard_map(
        shards,
        mesh=mesh,
        in_specs=(
            P("dp", "ctx", "head"),
            P("dp", "ctx", "head"),
            P("dp", "ctx", "head"),
            P("dp", "head", "ctx"),
            P(("ctx", "dp"), "head", None),
            P("dp", "ctx", None),
        ),
        out_specs=(
            P("dp", "ctx", "head"),
            P("dp", "ctx", "head"),
            P("dp", "ctx", "head"),
            P("dp", "ctx", "head"),
            P(("ctx", "dp"), "head", None),
        ),
        check_vma=False,
    )
```

```python
import functools

import jax
import jax.numpy as jnp
from jax import lax
from jax.experimental import pallas as pl
from jax.experimental.pallas import tpu as pltpu
from jax.sharding import PartitionSpec as P

DH = 128
SCALE = 1.0 / DH
F32 = jnp.float32
BF16 = jnp.bfloat16
EXTRA = 16
C_HOLD, C_JOIN, C26, C17, C20, C24 = 1070000000, 1070000000, 642000000, 1284000000, 642000000, 2140000000


def contract(a, b, dim_a, dim_b):
    return lax.dot_general(a, b, (((dim_a,), (dim_b,)), ((), ())), preferred_element_type=F32)


def head(ref, h):
    return ref[:, h * DH : (h + 1) * DH]


def call(kernel, out_shape, *args, staged=(), free_in=(), scratch=(), after=(), room=24, work=0):
    outs = list(out_shape) if isinstance(out_shape, (list, tuple)) else [out_shape]
    n, waits, count, made = len(args), len(after), len(staged), len(outs)

    def body(*refs):
        ins, rest = list(refs[:n]), refs[n + waits :]
        results, rest = rest[: made + 1], rest[made + 1 :]
        rest, buffers, sem = rest[: len(rest) - count - 1], rest[len(rest) - count - 1 : -1], rest[-1]
        copies = [pltpu.make_async_copy(ins[i], buffers[j], sem.at[j]) for j, i in enumerate(staged)]
        for copy in copies:
            copy.start()
        results[-1][...] = jnp.zeros_like(results[-1])
        for copy in copies:
            copy.wait()
        for j, i in enumerate(staged):
            ins[i] = buffers[j]
        kernel(*ins, *results[:-1], *rest)

    anywhere, local, far = (pl.BlockSpec(memory_space=m) for m in (pl.ANY, pltpu.VMEM, pltpu.HBM))
    results = pl.pallas_call(
        body,
        name=getattr(kernel, "func", kernel).__name__,
        out_shape=[*outs, struct((8, 128), F32)],
        in_specs=[far if i in staged or i in free_in else local for i in range(n)] + [anywhere] * waits,
        out_specs=[local] * (made + 1),
        scratch_shapes=[
            *scratch,
            *[pltpu.VMEM(args[i].shape, args[i].dtype) for i in staged],
            pltpu.SemaphoreType.DMA((max(count, 1),)),
        ],
        compiler_params=pltpu.CompilerParams(vmem_limit_bytes=room * 1024 * 1024),
        cost_estimate=pl.CostEstimate(flops=work, bytes_accessed=0, transcendentals=0),
    )(*args, *after)
    return (results[:-1] if isinstance(out_shape, (list, tuple)) else results[0]), results[-1]


def struct(shape, dtype):
    return jax.ShapeDtypeStruct(shape, dtype)


def store_decay(out_ref, total, groups):
    decay = jnp.broadcast_to(jnp.exp(total), (groups, DH))
    high = decay.astype(BF16).astype(F32)
    both = jnp.concatenate([high, decay - high], axis=0)
    out_ref[groups * DH : groups * DH + EXTRA, :] = both.astype(BF16)


def load_decay(ref, groups):
    both = ref[groups * DH : groups * DH + EXTRA, :].astype(F32)
    return both[:groups] + both[groups:]


def entering(refs, groups, forward):
    if lax.axis_size("ctx") == 4:
        near, far = refs
        bit = side(forward)
        decay = load_decay(near, groups) * bit + (1.0 - bit)
        row = (lax.axis_index("ctx") // 2).astype(F32)
        decay = decay * (row if forward else 1.0 - row)
        return lambda h: rows_of(near, h) * bit + decay[h : h + 1, :] * rows_of(far, h)
    decays = [load_decay(ref, groups) for ref in refs[:-1]]

    def state(h):
        total = rows_of(refs[-1], h)
        for ref, decay in zip(refs[-2::-1], decays[::-1]):
            total = rows_of(ref, h) + decay[h : h + 1, :] * total
        return total

    return state


def rows_of(ref, h):
    return ref[h * DH : (h + 1) * DH, :].astype(F32)


def side(forward):
    bit = lax.rem(lax.axis_index("ctx"), 2).astype(F32)
    return bit if forward else 1.0 - bit


def pair_kernel(groups, forward, own_ref, near_ref, *refs):
    out_ref = refs[-1]
    if len(refs) == 3:
        refs[1][...] = refs[0][...]
    bit = side(forward)
    own_decay, near_decay = load_decay(own_ref, groups), load_decay(near_ref, groups)
    for h in range(groups):
        here = slice(h, h + 1)
        own, near = rows_of(own_ref, h), rows_of(near_ref, h)
        own_share = bit + (1.0 - bit) * near_decay[here]
        near_share = bit * own_decay[here] + (1.0 - bit)
        out_ref[h * DH : (h + 1) * DH, :] = (own_share * own + near_share * near).astype(BF16)


def lower_mask(size):
    return lax.broadcasted_iota(jnp.int32, (size, size), 0) >= lax.broadcasted_iota(
        jnp.int32, (size, size), 1
    )


def ring_columns(w_ref, out_ref, hops, sem):
    width = w_ref.shape[1] // lax.axis_size("head")
    copies = []
    for j in range(out_ref.shape[1] // width):
        here = pl.ds(j * width, width)
        copies.append(pltpu.make_async_copy(w_ref.at[:, columns_after(hops + j, width)], out_ref.at[:, here], sem.at[j]))
        copies[-1].start()
    return copies


def sums(ld_ref, mask, rows):
    groups, left, terms = ld_ref.shape[0], ld_ref[...], []
    for _ in range(3):
        terms.append(left.astype(BF16))
        left = left - terms[-1].astype(F32)
    terms = jnp.concatenate([term.astype(F32) for term in terms], axis=0).astype(BF16)
    lower = mask.astype(F32).astype(BF16)
    if rows:
        total = contract(lower, terms, 1, 1)
        return total[:, :groups] + total[:, groups : 2 * groups] + total[:, 2 * groups :]
    total = contract(terms, lower, 1, 1)
    return total[:groups] + total[groups : 2 * groups] + total[2 * groups :]


def contrib_kernel(groups, k_hbm, v_hbm, ld_hbm, w_ref, state_ref, first_ref, rest_ref, k_ref, v_ref, ld_ref, sem, w_sem):
    moves = [
        pltpu.make_async_copy(source, held, sem.at[i])
        for i, (source, held) in enumerate(((ld_hbm, ld_ref), (k_hbm, k_ref), (v_hbm, v_ref)))
    ]
    for move in moves:
        move.start()
    count = first_ref.shape[1] * lax.axis_size("head") // w_ref.shape[1]
    copies = ring_columns(w_ref, first_ref, 1, w_sem)
    copies += ring_columns(w_ref, rest_ref, 1 + count, w_sem.at[pl.ds(count, w_sem.shape[0] - count)])
    moves[0].wait()
    size = k_ref.shape[0]
    mask = lower_mask(size)
    col = sums(ld_ref, mask, True)
    tail = jnp.exp(col[size - 1 :, :] - col)
    store_decay(state_ref, jnp.sum(ld_ref[...], axis=1, keepdims=True), groups)
    moves[1].wait()
    moves[2].wait()
    for h in range(groups):
        weighted = (head(k_ref, h).astype(F32) * tail[:, h : h + 1]).astype(BF16)
        state_ref[h * DH : (h + 1) * DH, :] = contract(weighted, head(v_ref, h), 0, 0).astype(BF16)
    for copy in copies:
        copy.wait()


def again_kernel(ref, again_ref):
    again_ref[...] = ref[...]


def intra_kernel(groups, q_ref, k_ref, v_ref, ld_ref, row_ref, col_ref, intra_ref):
    mask = lower_mask(q_ref.shape[0])
    row_ref[...] = sums(ld_ref, mask, False)
    col_ref[...] = sums(ld_ref, mask, True)
    for h in range(groups):
        probs = probs_of(q_ref, k_ref, spread_weights(row_ref, col_ref, mask, h), h)
        intra_ref[:, h * DH : (h + 1) * DH] = contract(probs, head(v_ref, h), 1, 0)


def probs_of(q_ref, k_ref, weights, h):
    return (contract(head(q_ref, h), head(k_ref, h), 1, 1) * SCALE * weights).astype(BF16)


def spread_weights(row_ref, col_ref, lower, h):
    spread = col_ref[:, h : h + 1] - row_ref[h : h + 1, :]
    return jnp.exp(jnp.where(lower, spread, -jnp.inf))


def attended_kernel(groups, count, *refs):
    states = refs[:count]
    q_ref, intra_ref, col_ref, pick_own_ref, pick_other_ref, g_ref = refs[count : count + 6]
    own_ref, other_ref, low_ref, held_ref, attended_ref, sem = refs[count + 6 :]
    copy = pltpu.make_async_copy(g_ref, held_ref, sem.at[0])
    copy.start()
    state = entering(states, groups, True)
    factor = jnp.exp(col_ref[...]) * SCALE
    for h in range(groups):
        low = state(h).astype(BF16)
        low_ref[h] = low
        inter = contract(head(q_ref, h), low, 1, 0)
        attended_ref[:, h * DH : (h + 1) * DH] = (
            head(intra_ref, h) + inter * factor[:, h : h + 1]
        ).astype(BF16)
    own_ref[...] = contract(attended_ref[...], pick_own_ref[...], 1, 0).astype(BF16)
    other_ref[...] = contract(attended_ref[...], pick_other_ref[...], 1, 0).astype(BF16)
    copy.wait()


def back_contrib_kernel(
    groups, own_ref, other_ref, pick_own_ref, pick_other_ref, q_ref, row_ref, col_ref, grad_ref, state_ref
):
    grad_ref[...] = (
        contract(own_ref[...], pick_own_ref[...], 1, 1) + contract(other_ref[...], pick_other_ref[...], 1, 1)
    ).astype(BF16)
    factor = jnp.exp(col_ref[...]) * SCALE
    for h in range(groups):
        weighted = (head(q_ref, h).astype(F32) * factor[:, h : h + 1]).astype(BF16)
        state_ref[h * DH : (h + 1) * DH, :] = contract(weighted, head(grad_ref, h), 0, 0).astype(BF16)
    store_decay(state_ref, row_ref[:, -1:], groups)


def back_key_kernel(groups, grad_ref, q_ref, v_ref, row_ref, col_ref, dprobs_ref, kpart_ref):
    lower = lower_mask(q_ref.shape[0])
    for h in range(groups):
        weights = spread_weights(row_ref, col_ref, lower, h)
        dprobs = (contract(head(grad_ref, h), head(v_ref, h), 1, 1) * SCALE * weights).astype(BF16)
        dprobs_ref[h] = dprobs
        kpart_ref[:, h * DH : (h + 1) * DH] = contract(dprobs, head(q_ref, h), 0, 0)


def back_query_kernel(groups, grad_ref, q_ref, k_ref, row_ref, col_ref, low_ref, dprobs_ref, qgrad_ref, vpart_ref):
    lower = lower_mask(q_ref.shape[0])
    factor = jnp.exp(col_ref[...]) * SCALE
    for h in range(groups):
        here = slice(h * DH, (h + 1) * DH)
        grad = head(grad_ref, h)
        qgrad_ref[:, here] = (
            contract(dprobs_ref[h], head(k_ref, h), 1, 0)
            + contract(grad, low_ref[h], 1, 1) * factor[:, h : h + 1]
        ).astype(BF16)
        probs = probs_of(q_ref, k_ref, spread_weights(row_ref, col_ref, lower, h), h)
        vpart_ref[:, here] = contract(probs, grad, 0, 0)


def back_inter_kernel(groups, count, *refs):
    states = refs[:count]
    k_ref, v_ref, col_ref, kpart_ref, vpart_ref, kgrad_ref, vgrad_ref = refs[count:]
    state = entering(states, groups, False)
    col = col_ref[...]
    tail = jnp.exp(col[col.shape[0] - 1 :, :] - col)
    for h in range(groups):
        here = slice(h * DH, (h + 1) * DH)
        low = state(h).astype(BF16)
        kgrad_ref[:, here] = (
            head(kpart_ref, h) + tail[:, h : h + 1] * contract(head(v_ref, h), low, 1, 1)
        ).astype(BF16)
        vgrad_ref[:, here] = (
            head(vpart_ref, h) + tail[:, h : h + 1] * contract(head(k_ref, h), low, 1, 0)
        ).astype(BF16)


def hops_of(state, forward):
    devices = lax.axis_size("ctx")
    out = []
    for hop in range(1, devices):
        if forward:
            pairs = [(i, i + hop) for i in range(devices - hop)]
        else:
            pairs = [(i + hop, i) for i in range(devices - hop)]
        out.append(lax.ppermute(state, "ctx", pairs))
    return out


def swapped(array):
    return lax.ppermute(array, "dp", [(0, 1), (1, 0)])


def flipped(array, bit):
    return lax.ppermute(array, "ctx", [(i, i ^ bit) for i in range(4)])


def rows_kernel(upper, ref, out_ref):
    half = out_ref.shape[0]
    out_ref[...] = ref[:half] if upper else ref[half:]


def join_kernel(*refs):
    lay_out(refs[:-1], refs[-1])


def lay_out(pieces, out_ref, columns=slice(None)):
    top = 0
    for piece in pieces:
        out_ref[top : top + piece.shape[0], :] = piece[:, columns]
        top += piece.shape[0]


def along(place):
    return place ^ (place >> 1) if lax.axis_size("head") == 4 else place


def columns_after(hops, width):
    devices = lax.axis_size("head")
    device = along(lax.rem(along(lax.axis_index("head")) + hops, devices))
    return pl.ds(pl.multiple_of(device * width, width), width)


def mix_kernel(count, place, splits, a_own, a_other, *refs):
    pieces, owns, others, w_ref = refs[:count], refs[count : -1 - splits], refs[-1 - splits : -1], refs[-1]
    width = w_ref.shape[1]
    away = []
    for j, own in enumerate(owns):
        lay_out(pieces, w_ref, slice((place + j) * width, (place + j + 1) * width))
        own[...] = contract(a_own[...], w_ref[...], 1, 0)
        away.append(contract(a_other[...], w_ref[...], 1, 0).astype(BF16))
    away = away[0] if len(away) == 1 else jnp.concatenate(away, axis=1)
    for i, other in enumerate(others):
        other[...] = away[:, i * other.shape[1] : (i + 1) * other.shape[1]]


def grad_kernel(top, count, earlier, g_own, g_other, first_ref, *refs):
    pieces, before, (own, other, w_ref) = refs[:count], refs[count : count + earlier], refs[count + earlier :]
    heads = lax.axis_size("head")
    rows, left, width = w_ref.shape[0], first_ref.shape[1], w_ref.shape[1] // heads
    w_ref[:, :left] = first_ref[top : top + rows]
    lay_out(pieces, w_ref.at[:, left:])
    for g_ref, old, out in ((g_own, before[:1], own), (g_other, before[1:], other)):
        total = None
        for j in range(heads):
            term = contract(
                g_ref[:, columns_after(1 + j, width)], w_ref[:, j * width : (j + 1) * width], 1, 1
            )
            total = term if total is None else total + term
        start = out.shape[1] - rows
        if old:
            out[:, :start] = old[0][...]
        out[:, start:] = total.astype(BF16)


def weight_kernel(blocks, a_own, a_other, g_own, g_other, *outs):
    rows = a_own.shape[1] // 4
    for stack, out in zip(blocks, outs):
        for i, (k, left, right) in enumerate(stack):
            here = slice(k * rows, (k + 1) * rows)
            out[i * rows : (i + 1) * rows] = (
                contract(a_own[:, here], g_own[:, left:right], 0, 0)
                + contract(a_other[:, here], g_other[:, left:right], 0, 0)
            ).astype(out.dtype)


def onward_kernel(mid_ref, far_ref, out_ref):
    out_ref[...] = (mid_ref[...] + far_ref[: mid_ref.shape[0]].astype(F32)).astype(BF16)


def total_kernel(own_ref, left_ref, right_ref, out_ref):
    rows, half = own_ref.shape[0], own_ref.shape[1] // 2
    for here, ref in ((slice(0, half), left_ref), (slice(half, 2 * half), right_ref)):
        out_ref[:, here] = own_ref[:, here] + ref[ref.shape[0] - rows :].astype(F32)


def ring_kernel(j, count, own_ref, *refs):
    width = own_ref.shape[1]
    other = [ref[...] for ref in refs[:count]]
    other = other[0] if count == 1 else jnp.concatenate(other, axis=1)
    total = own_ref[...] + other[:, j * width : (j + 1) * width].astype(F32)
    if len(refs) == count + 2:
        total = total + refs[count][...].astype(F32)
    refs[-1][...] = total.astype(BF16)


def passed(array):
    devices = lax.axis_size("head")
    pairs = [(along(i), along((i - 1) % devices)) for i in range(devices)]
    return lax.ppermute(array, "head", pairs)


def picks_kernel(groups, rows_each, own_ref, other_ref):
    devices, mine, core = lax.axis_size("ctx"), lax.axis_index("ctx"), lax.axis_index("dp")
    width = own_ref.shape[1]
    shape = (DH, width)
    feature, place = lax.broadcasted_iota(jnp.int32, shape, 0), lax.broadcasted_iota(jnp.int32, shape, 1)
    block = place // (rows_each * groups)
    if devices == 4:
        block = block ^ mine
    row = (place // groups) % rows_each
    for p, ref in ((core, own_ref), (1 - core, other_ref)):
        match = feature == (block * 2 + p) * rows_each + row
        for h in range(groups):
            ref[h * DH : (h + 1) * DH, :] = (match & (place % groups == h)).astype(F32).astype(BF16)


def shards(queries, keys, values, log_decay, w_out, grad_out):
    groups = log_decay.shape[1]
    size = queries.shape[1]
    devices, heads = lax.axis_size("ctx"), lax.axis_size("head")
    four = devices == 4
    q, k, v, ld, g = queries[0], keys[0], values[0], log_decay[0], grad_out[0]
    rows_each, _, width = w_out.shape
    rows, part, middle = rows_each * groups, width // heads, width // 2
    w = w_out.reshape(rows, width)
    features = groups * DH
    state_shape = struct((features + EXTRA, DH), BF16)
    flat = lambda dtype: struct((size, features), dtype)
    half = struct((size, features // 2), BF16)
    last = []

    def step(kernel, out_shape, *args, after=(), **kwargs):
        out, done = call(kernel, out_shape, *args, after=[*last, *after], **kwargs)
        last[:] = [done]
        return out

    near_heads = heads // 2
    first_shape, rest_shape = (struct((rows, count * part), BF16) for count in (near_heads, heads - near_heads))
    state, w_first, w_rest = step(
        functools.partial(contrib_kernel, groups),
        [state_shape, first_shape, rest_shape],
        k,
        v,
        ld,
        w,
        free_in=(0, 1, 2, 3),
        scratch=[
            *[pltpu.VMEM(array.shape, array.dtype) for array in (k, v, ld)],
            pltpu.SemaphoreType.DMA((3,)),
            pltpu.SemaphoreType.DMA((heads,)),
        ],
        room=60,
    )
    g_other = swapped(g)
    if four:
        near = flipped(state, 1)
        first_two, first_one = flipped(w_first, 2), flipped(w_first, 1)
        state = step(again_kernel, state_shape, state)
        pair = step(functools.partial(pair_kernel, groups, True), struct((features, DH), BF16), state, near)
        before = [near, flipped(pair, 2)]
        lower = lambda array: struct((rows // 2, array.shape[1]), BF16)
    pick_own, pick_other = step(
        functools.partial(picks_kernel, groups, rows_each),
        [struct((features, features // 2), BF16)] * 2,
        after=[g_other],
    )
    row, col, intra = step(
        functools.partial(intra_kernel, groups),
        (struct((groups, size), F32), struct((size, groups), F32), flat(F32)),
        q,
        k,
        v,
        ld,
    )
    if four:
        on_two = step(functools.partial(rows_kernel, True), lower(w_first), first_two)
        on_one = step(functools.partial(rows_kernel, False), lower(w_first), first_one)
        w_again = step(again_kernel, rest_shape, w_rest)
        first = [w_first, first_one, first_two, flipped(on_two, 1), flipped(on_one, 2)]
    else:
        before = hops_of(state, True)
        first = lax.all_gather(w_first, "ctx", axis=0, tiled=True)
        rest = [lax.all_gather(w_rest, "ctx", axis=0, tiled=True)]
    a_own, a_away, low, g_own = step(
        functools.partial(attended_kernel, groups, len(before)),
        (half, half, struct((groups, DH, DH), BF16), struct(g.shape, BF16)),
        *before,
        q,
        intra,
        col,
        pick_own,
        pick_other,
        g,
        free_in=(len(before) + 5,),
        scratch=[pltpu.VMEM((size, features), BF16), pltpu.SemaphoreType.DMA((1,))],
    )
    a_other = swapped(a_away)
    if four:
        first[3] = step(again_kernel, lower(w_first), first[3], work=C_HOLD)
        first = step(join_kernel, struct((devices * rows, first_shape.shape[1]), BF16), *first, work=C_JOIN)
    held = pltpu.VMEM((features // 2, part), BF16)

    def mix(pieces, place, count, splits=1, work=0):
        out = step(
            functools.partial(mix_kernel, len(pieces), place, splits),
            [struct((size, part), F32)] * count + [struct((size, count * part // splits), BF16)] * splits,
            a_own,
            a_other,
            *pieces,
            scratch=[held],
            work=work,
        )
        away = [swapped(other) for other in out[count:]]
        return [(own, away, j) for j, own in enumerate(out[:count])]

    def ring(terms, *arrived, work=0):
        own, away, j = terms
        return step(
            functools.partial(ring_kernel, j, len(away)), struct((size, part), BF16), own, *away, *arrived, work=work
        )

    def weights(blocks, shapes):
        return step(functools.partial(weight_kernel, blocks), shapes, a_own, a_other, g_own, g_other)

    def grad_of(pieces, top, *earlier):
        here = sum(piece.shape[0] for piece in pieces)
        wide = here + sum(array.shape[1] for array in earlier[:1])
        return step(
            functools.partial(grad_kernel, top, len(pieces), len(earlier)),
            [struct((size, wide), BF16)] * 2,
            g_own,
            g_other,
            first,
            *pieces,
            *earlier,
            scratch=[pltpu.VMEM((here, width), BF16)],
        )

    terms = mix([first], 0, near_heads, 3 if four else 1)
    if four:
        small = lambda dtype: struct((rows, middle), dtype)
        left, right = (0, middle), (middle, width)
        blocks = [
            [(3, *left)], [(3, *right), (2, *right)], [(1, *left)], [(2, *left)], [(1, *right)], [(0, 0, width)],
        ]
        far_left, both_right, near_left, mid_left, mid_right, own_sum = weights(
            blocks,
            [small(BF16), struct((2 * rows, middle), BF16), small(BF16), small(F32), small(F32), struct((rows, width), F32)],
        )
    arrived = passed(ring(terms[0]))
    if four:
        rest_one, rest_two = flipped(w_again, 1), flipped(w_again, 2)
        on_two = step(functools.partial(rows_kernel, True), lower(w_rest), rest_two)
        on_one = step(functools.partial(rows_kernel, False), lower(w_rest), rest_one)
        rest = [w_rest, rest_one, rest_two, flipped(on_two, 1), flipped(on_one, 2)]
        far_left, both_right, near_left = flipped(far_left, 1), flipped(both_right, 2), flipped(near_left, 1)
        grad_own, grad_away = grad_of(rest[3:], 3 * rows, *grad_of(rest[:3], 0))
    else:
        grad_own, grad_away = grad_of(rest, 0)
    grad_other = swapped(grad_away)
    for j in range(1, near_heads):
        arrived = passed(ring(terms[j], arrived, work=C17))
    grad, back = step(
        functools.partial(back_contrib_kernel, groups),
        (flat(BF16), state_shape),
        grad_own,
        grad_other,
        pick_own,
        pick_other,
        q,
        row,
        col,
    )
    if four:
        near = flipped(back, 1)
    else:
        after = hops_of(back, False)
    if four:
        on_left = flipped(step(onward_kernel, small(BF16), mid_left, far_left), 2)
    terms = mix(rest, 0, 1)
    if four:
        pair = step(
            functools.partial(pair_kernel, groups, False), struct((features, DH), BF16), back, near, work=C20
        )
        after = [near, lax.ppermute(pair, "ctx", [(2, 0), (3, 1)])]
    dprobs, key_part = step(
        functools.partial(back_key_kernel, groups),
        (struct((groups, size, size), BF16), flat(F32)),
        grad,
        q,
        v,
        row,
        col,
    )
    for j in range(1, heads - near_heads):
        arrived = passed(ring(terms[0], arrived))
        if four and j == 1:
            on_right = flipped(step(onward_kernel, small(BF16), mid_right, both_right), 1)
        if j == 1:
            query_grad, value_part = step(
                functools.partial(back_query_kernel, groups),
                (flat(BF16), flat(F32)),
                grad,
                q,
                k,
                row,
                col,
                low,
                dprobs,
            )
        terms = mix(rest, j, 1, 2 if four else 1)
    if four:
        own_sum = step(total_kernel, struct((rows, width), F32), own_sum, near_left, both_right)
    key_grad, value_grad = step(
        functools.partial(back_inter_kernel, groups, len(after)),
        (flat(BF16), flat(BF16)),
        *after,
        k,
        v,
        col,
        key_part,
        value_part,
        work=C24,
    )
    mixed = ring(terms[0], arrived, work=C26)
    if four:
        w_grad = step(total_kernel, struct((rows, width), F32), own_sum, on_left, on_right)
    else:
        w_grad = contract(a_own, g, 0, 0) + contract(a_other, g_other, 0, 0)
        w_grad = lax.psum_scatter(w_grad.astype(BF16), "ctx", scatter_dimension=0, tiled=True).astype(F32)
    return (
        mixed[None],
        query_grad[None],
        key_grad[None],
        value_grad[None],
        w_grad.reshape(rows_each, groups, width),
    )


def solution(mesh):
    return jax.shard_map(
        shards,
        mesh=mesh,
        in_specs=(
            P("dp", "ctx", "head"),
            P("dp", "ctx", "head"),
            P("dp", "ctx", "head"),
            P("dp", "head", "ctx"),
            P(("ctx", "dp"), "head", None),
            P("dp", "ctx", None),
        ),
        out_specs=(
            P("dp", "ctx", "head"),
            P("dp", "ctx", "head"),
            P("dp", "ctx", "head"),
            P("dp", "ctx", "head"),
            P(("ctx", "dp"), "head", None),
        ),
        check_vma=False,
    )
```
